768 devices in a mesh: dom: 64 (over y, x, core), sub: 12 (over z).
Axes of the slice: x: 4, y: 8, z: 12, core: 2. Of those that a mesh axis runs over, the one named last changes fastest.
Arguments:
- geometry: bfloat16 [6, 512, 98304], P(None, None, ('dom', 'sub')), may hold values from -1.8 to 4, as said below
- load: float32 [512, 98304], P(None, ('dom', 'sub')), may hold values from -600 to 600
- cells: int32 [768, 128], P(('dom', 'sub')), may hold values from 0 to 127, each once within a row
Outputs:
- smoothed: float32 [512, 98304], P(None, ('dom', 'sub'))
The draws below stay inside these ranges and needn't reach their ends.
Inputs may be any that keep to these rules, and one draw needn't show every extreme that they name: `geometry`: at each node the matrix [[g0, g3, g4], [g3, g1, g5], [g4, g5, g2]] is symmetric positive definite.
All inputs are finite; a program needn't handle non-finite values.
Results may differ from the reference program's by a relative error of at most 0.0003.
Values sent between devices are 32-bit elements; how exact they have to be, the bound alone decides.
No kernel may reach another device: no remote copies, remote signals or barrier semaphores. Data moves between devices by JAX's collectives and lax.ppermute only.
A program may use at most 128 MiB of HBM per device.

```python
import jax
import jax.numpy as jnp
import numpy as np
from jax import lax

NP = 8
EZ = 8
APPLY = 4
E_DEV = 128
ELEMS = 98304
N_DOM = 64
N_SUB = 12


def draw_geometry(key, part):
    key = jax.random.fold_in(key, 11)
    keys = jax.random.split(key, 2)
    lower_end = 0.5
    upper_end = 2.0
    coupling = 0.4
    shape = (3, NP * NP * NP, ELEMS)
    diagonal = jnp.exp(jax.random.uniform(keys[0], shape, jnp.float32, jnp.log(lower_end), jnp.log(upper_end)))
    factor = jax.random.uniform(keys[1], shape, jnp.float32, -coupling, coupling)
    roots = jnp.sqrt(diagonal)
    coupled = factor * jnp.stack([roots[0] * roots[1], roots[0] * roots[2], roots[1] * roots[2]])
    return jnp.concatenate([diagonal, coupled], 0).astype(jnp.bfloat16)


def block_levels(key, extent, cuts, least, top_value):
    factor_of, own = 1.0, jax.random.fold_in(key, 6)
    for axis_at, blocks in cuts:
        draws = jnp.exp(jax.random.uniform(jax.random.fold_in(own, axis_at), (blocks,), jnp.float32, least / len(cuts), top_value / len(cuts)))
        factor_of = factor_of * jnp.repeat(draws, extent[axis_at] // blocks).reshape([-1 if axis == axis_at else 1 for axis in range(len(extent))])
    return factor_of


def centred(rng, dims, deviation, limit, shards=(), kind=jnp.bfloat16):
    array = deviation * jax.random.normal(rng, dims, jnp.float32)
    if shards:
        array = array * block_levels(rng, dims, shards, -0.22, 0.18)
    return jnp.clip(array, -limit, limit).astype(kind)


def setup_inputs(seed: int = 0) -> dict:
    splits = jax.random.split(jax.random.key(seed), 4)
    geometry = draw_geometry(jax.random.fold_in(splits[3], 71), 0)
    load = centred(splits[1], (NP * NP * NP, ELEMS), 100.0, 600.0, ((1, 768),), jnp.float32)
    cells = jax.vmap(lambda own: jax.random.permutation(own, E_DEV))(jax.random.split(splits[2], (N_DOM * N_SUB))).reshape((N_DOM * N_SUB, E_DEV)).astype(jnp.int32)
    return dict(geometry=geometry, load=load, cells=cells)


cheb_low = 0.4
cheb_high = 4.0


def legendre_values(points, degree):
    before = np.ones(points.shape[0])
    current = points.copy()
    if degree == 0:
        return before, before
    for order in range(2, degree + 1):
        following = ((2 * order - 1) * points * current - (order - 1) * before) / order
        before = current
        current = following
    return current, before


def derivative_table(number):
    degree = number - 1
    points = np.cos(np.pi * np.arange(degree + 1) / degree)
    for sweep in range(60):
        current, before = legendre_values(points, degree)
        inner = points[1:-1]
        step_size = (inner * current[1:-1] - before[1:-1]) / ((degree + 1) * current[1:-1])
        points = np.concatenate([points[:1], inner - step_size, points[-1:]])
    points = np.sort(points)
    points = np.concatenate([np.zeros(1) - 1.0, points[1:-1], np.zeros(1) + 1.0])
    values, unused = legendre_values(points, degree)
    matrix = np.zeros((number, number))
    for row_index in range(number):
        for col_index in range(number):
            if row_index != col_index:
                matrix[row_index, col_index] = values[row_index] / (values[col_index] * (points[row_index] - points[col_index]))
    matrix[0, 0] = -degree * (degree + 1) / 4.0
    matrix[degree, degree] = degree * (degree + 1) / 4.0
    return matrix


def element_apply(values_in, geometry_block, derivative):
    highest = lax.Precision.HIGHEST
    coeffs = [geometry_block[index].astype(jnp.float32) for index in range(6)]
    grad_r = jnp.einsum('ia,abc...->ibc...', derivative, values_in, precision=highest)
    grad_s = jnp.einsum('jb,abc...->ajc...', derivative, values_in, precision=highest)
    grad_t = jnp.einsum('kc,abc...->abk...', derivative, values_in, precision=highest)
    flux_r = coeffs[0] * grad_r + coeffs[3] * grad_s + coeffs[4] * grad_t
    flux_s = coeffs[3] * grad_r + coeffs[1] * grad_s + coeffs[5] * grad_t
    flux_t = coeffs[4] * grad_r + coeffs[5] * grad_s + coeffs[2] * grad_t
    summed = jnp.einsum('ai,abc...->ibc...', derivative, flux_r, precision=highest)
    summed = summed + jnp.einsum('bj,abc...->ajc...', derivative, flux_s, precision=highest)
    return summed + jnp.einsum('ck,abc...->abk...', derivative, flux_t, precision=highest)


def element_diagonal(geometry_block, derivative):
    highest = lax.Precision.HIGHEST
    coeffs = [geometry_block[index].astype(jnp.float32) for index in range(6)]
    square = derivative * derivative
    middle = jnp.diagonal(derivative)
    extra = (1,) * (coeffs[0].ndim - 3)
    d_first = middle.reshape((-1, 1, 1) + extra)
    d_second = middle.reshape((1, -1, 1) + extra)
    d_third = middle.reshape((1, 1, -1) + extra)
    summed = jnp.einsum('ai,abc...->ibc...', square, coeffs[0], precision=highest)
    summed = summed + jnp.einsum('bj,abc...->ajc...', square, coeffs[1], precision=highest)
    summed = summed + jnp.einsum('ck,abc...->abk...', square, coeffs[2], precision=highest)
    cross = d_first * d_second * coeffs[3] + d_first * d_third * coeffs[4] + d_second * d_third * coeffs[5]
    return summed + 2.0 * cross


def fold_axis(values_in, node_axis, cell_axis):
    reordered = jnp.moveaxis(values_in, (cell_axis, node_axis), (-2, -1))
    number = reordered.shape[-2]
    span = reordered.shape[-1] - 1
    prefix = reordered.shape[:-2]
    leading = reordered[..., :span].reshape(prefix + (number * span,))
    trailing = jnp.pad(reordered[..., span:], [(0, 0)] * len(prefix) + [(0, 0), (span - 1, 0)]).reshape(prefix + (number * span,))
    zeros_end = jnp.zeros(prefix + (1,), values_in.dtype)
    return jnp.concatenate([leading, zeros_end], -1) + jnp.concatenate([zeros_end, trailing], -1)


def spread_axis(values_in, axis_pos, span):
    reordered = jnp.moveaxis(values_in, axis_pos, -1)
    number = (reordered.shape[-1] - 1) // span
    prefix = reordered.shape[:-1]
    leading = reordered[..., :number * span].reshape(prefix + (number, span))
    trailing = reordered[..., span::span][..., None]
    return jnp.concatenate([leading, trailing], -1)


def elements_to_grid(elements):
    folded = fold_axis(elements, 0, 3)
    folded = fold_axis(folded, 0, 2)
    return fold_axis(folded, 0, 1)


def grid_to_elements(field_grid, span):
    spread = spread_axis(field_grid, 0, span)
    spread = spread_axis(spread, 0, span)
    spread = spread_axis(spread, 0, span)
    return spread.transpose(1, 3, 5, 0, 2, 4)


def smooth(right_side, diagonal, operate):
    centre = 0.5 * (cheb_high + cheb_low)
    half_width = 0.5 * (cheb_high - cheb_low)
    ratio = centre / half_width
    rho_now = 1.0 / ratio
    residual = right_side
    direction = residual / diagonal / centre
    iterate = direction
    for step in range(APPLY):
        residual = residual - operate(direction)
        rho_new = 1.0 / (2.0 * ratio - rho_now)
        direction = (rho_new * rho_now) * direction + (2.0 * rho_new / half_width) * (residual / diagonal)
        iterate = iterate + direction
        rho_now = rho_new
    return iterate


def to_devices(global_elements):
    shaped = global_elements.reshape(NP, NP, NP, N_DOM, 4, N_SUB, 4, EZ)
    return shaped.transpose(3, 5, 0, 1, 2, 4, 6, 7).reshape(N_DOM * N_SUB, NP, NP, NP, 4, 4, EZ)


def from_devices(per_device):
    shaped = per_device.reshape(N_DOM, N_SUB, NP, NP, NP, 4, 4, EZ)
    return shaped.transpose(2, 3, 4, 0, 5, 1, 6, 7).reshape(NP, NP, NP, 4 * N_DOM, 4 * N_SUB, EZ)


def reference(geometry, load, cells):
    derivative = jnp.asarray(derivative_table(NP), jnp.float32)
    span = NP - 1
    devices = N_DOM * N_SUB
    arange_row = jnp.arange(E_DEV, dtype=jnp.int32)
    inverse = jax.vmap(lambda listed: jnp.zeros(E_DEV, jnp.int32).at[listed].set(arange_row))(cells)
    geo_listed = geometry.reshape(6, NP ** 3, devices, E_DEV)
    geo_sorted = jnp.take_along_axis(geo_listed, inverse[None, None], axis=3)
    geo_blocks = geo_sorted.transpose(2, 0, 1, 3).reshape(devices, 6, NP, NP, NP, 4, 4, EZ)
    load_listed = load.reshape(NP ** 3, devices, E_DEV)
    load_sorted = jnp.take_along_axis(load_listed, inverse[None], axis=2)
    load_blocks = load_sorted.transpose(1, 0, 2).reshape(devices, NP, NP, NP, 4, 4, EZ)

    def operate(field_grid):
        elements = to_devices(grid_to_elements(field_grid, span))
        images = lax.map(lambda pair: element_apply(pair[0], pair[1], derivative), (elements, geo_blocks))
        return elements_to_grid(from_devices(images))

    diag_blocks = lax.map(lambda block: element_diagonal(block, derivative), geo_blocks)
    right_side = elements_to_grid(from_devices(load_blocks))
    diagonal = elements_to_grid(from_devices(diag_blocks))
    iterate = smooth(right_side, diagonal, operate)
    per_device = to_devices(grid_to_elements(iterate, span)).reshape(devices, NP ** 3, E_DEV)
    listed = jnp.take_along_axis(per_device, cells[:, None, :], axis=2)
    return listed.transpose(1, 0, 2).reshape(NP ** 3, ELEMS)
```

```python
import functools

import jax
import jax.numpy as jnp
import ml_dtypes
import numpy as np
from jax import lax
from jax.experimental import pallas as pl
from jax.experimental.pallas import tpu as pltpu
from jax.sharding import PartitionSpec as P

NP = 8
APPLY = 4
LANES = 128
ROWS = NP**3

cheb_low = 0.4
cheb_high = 4.0


def legendre_values(points, degree):
    before = np.ones(points.shape[0])
    current = points.copy()
    for order in range(2, degree + 1):
        following = ((2 * order - 1) * points * current - (order - 1) * before) / order
        before = current
        current = following
    return (current, before)


def derivative_table(number):
    degree = number - 1
    points = np.cos(np.pi * np.arange(degree + 1) / degree)
    for sweep in range(60):
        current, before = legendre_values(points, degree)
        inner = points[1:-1]
        step_size = (inner * current[1:-1] - before[1:-1]) / ((degree + 1) * current[1:-1])
        points = np.concatenate([points[:1], inner - step_size, points[-1:]])
    points = np.sort(points)
    points = np.concatenate([np.zeros(1) - 1.0, points[1:-1], np.zeros(1) + 1.0])
    values, unused = legendre_values(points, degree)
    matrix = np.zeros((number, number))
    for row_index in range(number):
        for col_index in range(number):
            if row_index != col_index:
                matrix[row_index, col_index] = values[row_index] / (
                    values[col_index] * (points[row_index] - points[col_index])
                )
    matrix[0, 0] = -degree * (degree + 1) / 4.0
    matrix[degree, degree] = degree * (degree + 1) / 4.0
    return matrix


def three_products(matrix):
    matrix = matrix.astype(np.float32)
    high = matrix.astype(ml_dtypes.bfloat16)
    low = (matrix - high.astype(np.float32)).astype(ml_dtypes.bfloat16)
    return np.concatenate([high, high, low], axis=1)


def tables():
    derivative = derivative_table(NP).astype(np.float32).astype(np.float64)
    eye = np.eye(NP)
    outer = three_products(np.kron(derivative, eye))
    inner = three_products(np.kron(eye, derivative))
    outer_t = three_products(np.kron(derivative.T, eye))
    inner_t = three_products(np.kron(eye, derivative.T))
    apply_table = np.concatenate([outer, inner, outer_t, inner_t], axis=0)
    square = derivative * derivative
    diag_table = np.concatenate(
        [three_products(np.kron(square.T, eye)), three_products(np.kron(eye, square.T))], axis=0
    )
    return apply_table, diag_table, np.diagonal(derivative)


def split_rows(values):
    high = values.astype(jnp.bfloat16)
    low = (values - high.astype(jnp.float32)).astype(jnp.bfloat16)
    return jnp.concatenate([high, low, high], axis=0)


def multiply(left, right):
    return jnp.dot(left, right, preferred_element_type=jnp.float32)


def gather_first(ref, j):
    return jnp.concatenate([ref[i * 64 + j * 8 : i * 64 + j * 8 + 8, :] for i in range(NP)], axis=0)


def lane_of(rows):
    return lax.broadcasted_iota(jnp.int32, (rows, LANES), 1)


def join_pair(low_face, high_face, lane, unit, number):
    coordinate = (lane // unit) % number
    new_low = low_face + jnp.where(coordinate > 0, pltpu.roll(high_face, unit, 1), 0.0)
    new_high = high_face + jnp.where(
        coordinate < number - 1, pltpu.roll(low_face, LANES - unit, 1), 0.0
    )
    return new_low, new_high


def join_local(ref):
    lane8 = lane_of(8)
    lane64 = lane_of(64)
    for i in range(NP):
        first = slice(i * 64, i * 64 + 8)
        last = slice(i * 64 + 56, i * 64 + 64)
        ref[first, :], ref[last, :] = join_pair(ref[first, :], ref[last, :], lane8, 8, 4)
    ref[0:64, :], ref[448:512, :] = join_pair(ref[0:64, :], ref[448:512, :], lane64, 32, 4)
    first = pl.ds(0, 64, stride=8)
    last = pl.ds(7, 64, stride=8)
    new_first, new_last = join_pair(ref[first, :], ref[last, :], lane64, 1, 8)
    ref[first, :] = new_first
    ref[last, :] = new_last


class Side:
    def __init__(self, sizes, stage):
        a = lax.axis_index("dom")
        b = lax.axis_index("sub")
        self.lr = lax.rem(a + stage, 2)
        self.ls = lax.rem(b + stage, 2)
        self.place = 2 * self.lr + self.ls
        self.dom_slot = 2 * (1 - self.lr) + self.ls
        self.sub_slot = 2 * self.lr + (1 - self.ls)
        self.far_slot = 3 - self.place
        self.vr = None
        self.vs = None
        if stage:
            self.vr = jnp.where(self.lr == 1, a > 0, a < sizes[0] - 1)
            self.vs = jnp.where(self.ls == 1, b > 0, b < sizes[1] - 1)
        self.i_row = pl.multiple_of((1 - self.lr) * 448, 64)
        self.j_row = (1 - self.ls) * 56


def keep(mask, *conditions):
    for condition in conditions:
        if condition is not None:
            mask = jnp.logical_and(mask, condition)
    return mask


def pack_faces(ref, side):
    lane = lane_of(16)
    dom_face = jnp.zeros((16, LANES), jnp.float32)
    sub_face = jnp.zeros((16, LANES), jnp.float32)
    for g in range(4):
        block = ref[pl.ds(pl.multiple_of(side.i_row + g * 16, 8), 16), :]
        shift = (g * 32 + 32 * (1 - side.lr)) & 127
        dom_face = jnp.where(lane // 32 == g, pltpu.roll(block, shift, 1), dom_face)
        block = jnp.concatenate(
            [
                ref[pl.ds(pl.multiple_of(i * 64 + side.j_row, 8), 8), :]
                for i in (2 * g, 2 * g + 1)
            ],
            axis=0,
        )
        shift = (g * 8 + 128 - 24 * (1 - side.ls)) & 127
        sub_face = jnp.where((lane // 8) % 4 == g, pltpu.roll(block, shift, 1), sub_face)
    corner = ref[pl.ds(pl.multiple_of(side.i_row + side.j_row, 8), 8), :]
    return dom_face, sub_face, corner


def write_faces(out_ref, field, faces, side):
    dom_face, sub_face, corner = faces
    row = field * 16
    out_ref[side.dom_slot, row : row + 16, :] = dom_face
    out_ref[side.sub_slot, row : row + 16, :] = sub_face
    out_ref[side.far_slot, row : row + 8, :] = corner
    out_ref[side.far_slot, row + 8 : row + 16, :] = jnp.zeros((8, LANES), jnp.float32)
    out_ref[side.place, row : row + 16, :] = jnp.zeros((16, LANES), jnp.float32)


def add_faces(ref, recv_ref, field, side):
    lane = lane_of(16)
    lane8 = lane_of(8)
    row = field * 16
    dom_face = recv_ref[side.dom_slot, row : row + 16, :]
    for g in range(4):
        shift = (96 * (1 - side.lr) + 128 - g * 32) & 127
        mask = keep(lane // 32 == 3 * (1 - side.lr), side.vr)
        at = pl.ds(pl.multiple_of(side.i_row + g * 16, 8), 16)
        ref[at, :] = ref[at, :] + jnp.where(mask, pltpu.roll(dom_face, shift, 1), 0.0)
    sub_mask = keep((lane8 // 8) % 4 == 3 * (1 - side.ls), side.vs)
    sub_face = recv_ref[side.sub_slot, row : row + 16, :]
    for g in range(4):
        shift = (24 * (1 - side.ls) + 128 - g * 8) & 127
        rolled = pltpu.roll(sub_face, shift, 1)
        for part in range(2):
            at = pl.ds(pl.multiple_of((2 * g + part) * 64 + side.j_row, 8), 8)
            piece = rolled[part * 8 : part * 8 + 8, :]
            ref[at, :] = ref[at, :] + jnp.where(sub_mask, piece, 0.0)
    corner = recv_ref[side.far_slot, row : row + 8, :]
    offset = 96 * (1 - side.lr) + 24 * (1 - side.ls)
    shift = (2 * offset + 256 - 120) & 127
    mask = keep(lane8 // 8 == offset // 8, side.vr, side.vs)
    at = pl.ds(pl.multiple_of(side.i_row + side.j_row, 8), 8)
    ref[at, :] = ref[at, :] + jnp.where(mask, pltpu.roll(corner, shift, 1), 0.0)


def apply_operator(value_ref, geo_ref, table_ref, image_ref, work_ref):
    outer = table_ref[0:64, :]
    both = table_ref[0:128, :]
    outer_t = table_ref[128:192, :]
    inner_t = table_ref[192:256, :]
    for j in range(NP):
        product = multiply(outer, split_rows(gather_first(value_ref, j)))
        for i in range(NP):
            work_ref[i * 64 + j * 8 : i * 64 + j * 8 + 8, :] = product[i * 8 : i * 8 + 8, :]
    for i in range(NP):
        at = slice(i * 64, i * 64 + 64)
        product = multiply(both, split_rows(value_ref[at, :]))
        grad_r = work_ref[at, :]
        grad_s = product[0:64, :]
        grad_t = product[64:128, :]
        g = [geo_ref[index, at, :].astype(jnp.float32) for index in range(6)]
        work_ref[at, :] = g[0] * grad_r + g[3] * grad_s + g[4] * grad_t
        flux_s = g[3] * grad_r + g[1] * grad_s + g[5] * grad_t
        flux_t = g[4] * grad_r + g[5] * grad_s + g[2] * grad_t
        image_ref[at, :] = multiply(outer_t, split_rows(flux_s)) + multiply(
            inner_t, split_rows(flux_t)
        )
    for j in range(NP):
        product = multiply(outer_t, split_rows(gather_first(work_ref, j)))
        for i in range(NP):
            at = slice(i * 64 + j * 8, i * 64 + j * 8 + 8)
            image_ref[at, :] = image_ref[at, :] + product[i * 8 : i * 8 + 8, :]


def emit_faces(ref, field, send_ref, later_ref, sides):
    write_faces(send_ref, field, pack_faces(ref, sides[0]), sides[0])
    write_faces(later_ref, field, pack_faces(ref, sides[1]), sides[1])


def permute_exact(values, table):
    total = None
    for part in range(3):
        piece = values.astype(jnp.bfloat16)
        moved = multiply(piece, table)
        values = values - piece.astype(jnp.float32)
        total = moved if total is None else total + moved
    return total


def begin_kernel(sizes, middle, geo_ref, load_ref, cells_ref, table_ref, geo_out, parts_ref, send_ref, later_ref, work_ref):
    listed = cells_ref[...]
    cell = lax.broadcasted_iota(jnp.int32, (LANES, LANES), 0)
    by_cell = jnp.where(cell == jnp.broadcast_to(listed, (LANES, LANES)), 1.0, 0.0)
    table = by_cell.T.astype(jnp.bfloat16)
    for index in range(6):
        geo_out[index] = multiply(geo_ref[index], table).astype(jnp.bfloat16)
    outer = table_ref[0:64, :]
    inner = table_ref[64:128, :]
    work_ref[...] = geo_out[0].astype(jnp.float32)
    load_part = parts_ref.at[0]
    diag_part = parts_ref.at[1]
    sub_row = lax.broadcasted_iota(jnp.int32, (64, LANES), 0) % 8
    third = jnp.where(sub_row == 0, middle[0], jnp.where(sub_row == 7, middle[7], 0.0))
    for i in range(NP):
        at = slice(i * 64, i * 64 + 64)
        load_part[at, :] = permute_exact(load_ref[at, :], table)
        first = split_rows(geo_out[1, at, :].astype(jnp.float32))
        second = split_rows(geo_out[2, at, :].astype(jnp.float32))
        total = multiply(outer, first) + multiply(inner, second)
        if i in (0, 7):
            total = total + 2.0 * middle[i] * third * geo_out[4, at, :].astype(jnp.float32)
        diag_part[at, :] = total
        for j in (0, 7):
            here = slice(i * 64 + j * 8, i * 64 + j * 8 + 8)
            fifth = geo_out[5, at, :].astype(jnp.float32)[j * 8 : j * 8 + 8, :]
            extra = middle[j] * third[0:8, :] * fifth
            if i in (0, 7):
                cross = geo_out[3, at, :].astype(jnp.float32)[j * 8 : j * 8 + 8, :]
                extra = extra + middle[i] * middle[j] * cross
            diag_part[here, :] = diag_part[here, :] + 2.0 * extra
    for j in range(NP):
        product = multiply(outer, split_rows(gather_first(work_ref, j)))
        for i in range(NP):
            at = slice(i * 64 + j * 8, i * 64 + j * 8 + 8)
            diag_part[at, :] = diag_part[at, :] + product[i * 8 : i * 8 + 8, :]
    sides = (Side(sizes, 0), Side(sizes, 1))
    for field in range(2):
        join_local(parts_ref.at[field])
        emit_faces(parts_ref.at[field], field, send_ref, later_ref, sides)


def middle_kernel(sizes, fields, recv_ref, later_ref, out_ref):
    now = Side(sizes, 0)
    then = Side(sizes, 1)
    out_ref[...] = later_ref[...]
    lane = lane_of(8)
    for field in range(fields):
        row = field * 16

        def correct(slot_in, low_in, slot_out, low_out):
            piece = recv_ref[slot_in, pl.ds(pl.multiple_of(row + 8 * (1 - low_in), 8), 8), :]
            shift = (8 + 128 - 8 * (1 - low_out) + 8 * (1 - low_in) - 8) & 127
            mask = lane // 8 == 15 * (1 - low_out)
            at = pl.ds(pl.multiple_of(row + 8 * (1 - low_out), 8), 8)
            out_ref[slot_out, at, :] = out_ref[slot_out, at, :] + jnp.where(
                mask, pltpu.roll(piece, shift, 1), 0.0
            )

        correct(now.sub_slot, then.lr, then.dom_slot, now.ls)
        correct(now.dom_slot, then.ls, then.sub_slot, now.lr)


def coefficients():
    centre = 0.5 * (cheb_high + cheb_low)
    half_width = 0.5 * (cheb_high - cheb_low)
    ratio = centre / half_width
    rho_now = 1.0 / ratio
    steps = []
    for step in range(APPLY):
        rho_new = 1.0 / (2.0 * ratio - rho_now)
        steps.append((rho_new * rho_now, 2.0 * rho_new / half_width))
        rho_now = rho_new
    return centre, steps


def first_kernel(sizes, centre, parts_ref, recv_ref, recv2_ref, geo_ref, table_ref, residual_ref, diag_ref, direction_ref, image_ref, send_ref, later_ref, work_ref):
    sides = (Side(sizes, 0), Side(sizes, 1))
    residual_ref[...] = parts_ref[0]
    diag_ref[...] = parts_ref[1]
    for field, ref in ((0, residual_ref), (1, diag_ref)):
        add_faces(ref, recv_ref, field, sides[0])
        add_faces(ref, recv2_ref, field, sides[1])
    direction_ref[...] = residual_ref[...] / diag_ref[...] / centre
    apply_operator(direction_ref, geo_ref, table_ref, image_ref, work_ref)
    join_local(image_ref)
    emit_faces(image_ref, 0, send_ref, later_ref, sides)


def step_kernel(sizes, pair, part_ref, recv_ref, recv2_ref, geo_ref, table_ref, old_residual_ref, diag_ref, old_direction_ref, residual_ref, direction_ref, image_ref, send_ref, later_ref, work_ref):
    sides = (Side(sizes, 0), Side(sizes, 1))
    work_ref[...] = part_ref[...]
    add_faces(work_ref, recv_ref, 0, sides[0])
    add_faces(work_ref, recv2_ref, 0, sides[1])
    residual = old_residual_ref[...] - work_ref[...]
    residual_ref[...] = residual
    direction_ref[...] = pair[0] * old_direction_ref[...] + pair[1] * (residual / diag_ref[...])
    apply_operator(direction_ref, geo_ref, table_ref, image_ref, work_ref)
    join_local(image_ref)
    emit_faces(image_ref, 0, send_ref, later_ref, sides)


def end_kernel(sizes, pair, part_ref, recv_ref, recv2_ref, residual_ref, diag_ref, d0_ref, d1_ref, d2_ref, d3_ref, cells_ref, out_ref, work_ref):
    sides = (Side(sizes, 0), Side(sizes, 1))
    work_ref[...] = part_ref[...]
    add_faces(work_ref, recv_ref, 0, sides[0])
    add_faces(work_ref, recv2_ref, 0, sides[1])
    cell = lax.broadcasted_iota(jnp.int32, (LANES, LANES), 0)
    by_cell = jnp.where(cell == jnp.broadcast_to(cells_ref[...], (LANES, LANES)), 1.0, 0.0)
    table = by_cell.astype(jnp.bfloat16)
    for i in range(NP):
        at = slice(i * 64, i * 64 + 64)
        residual = residual_ref[at, :] - work_ref[at, :]
        last = d3_ref[at, :]
        direction = pair[0] * last + pair[1] * (residual / diag_ref[at, :])
        iterate = d0_ref[at, :] + d1_ref[at, :] + d2_ref[at, :] + last + direction
        out_ref[at, :] = permute_exact(iterate, table)


def call(kernel, outs, *operands, scratch=True, name=None):
    return pl.pallas_call(
        kernel,
        out_shape=outs,
        scratch_shapes=[pltpu.VMEM((ROWS, LANES), jnp.float32)] if scratch else [],
        compiler_params=pltpu.CompilerParams(vmem_limit_bytes=32 * 2**20),
        name=name,
    )(*operands)


def exchange_groups(sizes, stage):
    dom, sub = sizes
    groups = []
    for a in range(stage, dom + stage, 2):
        for b in range(stage, sub + stage, 2):
            groups.append(
                [((a + da) % dom) * sub + (b + db) % sub for da in (0, 1) for db in (0, 1)]
            )
    return groups


def solution(mesh):
    sizes = (mesh.shape["dom"], mesh.shape["sub"])
    apply_table, diag_table, middle = tables()
    middle = [float(value) for value in middle]
    centre, steps = coefficients()
    field = jax.ShapeDtypeStruct((ROWS, LANES), jnp.float32)
    one = jax.ShapeDtypeStruct((4, 16, LANES), jnp.float32)
    two = jax.ShapeDtypeStruct((4, 32, LANES), jnp.float32)

    def exchange(send, stage):
        return lax.all_to_all(
            send,
            ("dom", "sub"),
            0,
            0,
            axis_index_groups=exchange_groups(sizes, stage),
            tiled=True,
        )

    def assemble(send, later, fields):
        shape = one if fields == 1 else two
        recv = exchange(send, 0)
        send2 = call(
            functools.partial(middle_kernel, sizes, fields), shape, recv, later, scratch=False, name="faces"
        )
        return recv, exchange(send2, 1)

    def shards(geometry, load, cells):
        table = jnp.asarray(apply_table)
        geo, parts, send, later = call(
            functools.partial(begin_kernel, sizes, middle),
            (
                jax.ShapeDtypeStruct(geometry.shape, jnp.bfloat16),
                jax.ShapeDtypeStruct((2, ROWS, LANES), jnp.float32),
                two,
                two,
            ),
            geometry,
            load,
            cells,
            jnp.asarray(diag_table),
            name="begin",
        )
        recv, recv2 = assemble(send, later, 2)
        residual, diag, direction, image, send, later = call(
            functools.partial(first_kernel, sizes, centre),
            (field, field, field, field, one, one),
            parts,
            recv,
            recv2,
            geo,
            table,
            name="first",
        )
        directions = [direction]
        for pair in steps[:-1]:
            recv, recv2 = assemble(send, later, 1)
            residual, direction, image, send, later = call(
                functools.partial(step_kernel, sizes, pair),
                (field, field, field, one, one),
                image,
                recv,
                recv2,
                geo,
                table,
                residual,
                diag,
                direction,
                name="step",
            )
            directions.append(direction)
        recv, recv2 = assemble(send, later, 1)
        return call(
            functools.partial(end_kernel, sizes, steps[-1]),
            field,
            image,
            recv,
            recv2,
            residual,
            diag,
            *directions,
            cells,
            name="end",
        )

    placed = (P(None, None, ("dom", "sub")), P(None, ("dom", "sub")), P(("dom", "sub"), None))
    return jax.shard_map(
        shards, mesh=mesh, in_specs=placed, out_specs=P(None, ("dom", "sub")), check_vma=False
    )
```

```python
import functools

import jax
import jax.numpy as jnp
import ml_dtypes
import numpy as np
from jax import lax
from jax.experimental import pallas as pl
from jax.experimental.pallas import tpu as pltpu
from jax.sharding import PartitionSpec as P

NP = 8
APPLY = 4
ORDERS = ((0, 1),) * 5
LANES = 128
ROWS = NP**3

cheb_low = 0.4
cheb_high = 4.0


def legendre_values(points, degree):
    before = np.ones(points.shape[0])
    current = points.copy()
    for order in range(2, degree + 1):
        following = ((2 * order - 1) * points * current - (order - 1) * before) / order
        before = current
        current = following
    return (current, before)


def derivative_table(number):
    degree = number - 1
    points = np.cos(np.pi * np.arange(degree + 1) / degree)
    for sweep in range(60):
        current, before = legendre_values(points, degree)
        inner = points[1:-1]
        step_size = (inner * current[1:-1] - before[1:-1]) / ((degree + 1) * current[1:-1])
        points = np.concatenate([points[:1], inner - step_size, points[-1:]])
    points = np.sort(points)
    points = np.concatenate([np.zeros(1) - 1.0, points[1:-1], np.zeros(1) + 1.0])
    values, unused = legendre_values(points, degree)
    matrix = np.zeros((number, number))
    for row_index in range(number):
        for col_index in range(number):
            if row_index != col_index:
                matrix[row_index, col_index] = values[row_index] / (
                    values[col_index] * (points[row_index] - points[col_index])
                )
    matrix[0, 0] = -degree * (degree + 1) / 4.0
    matrix[degree, degree] = degree * (degree + 1) / 4.0
    return matrix


def three_products(matrix):
    matrix = matrix.astype(np.float32)
    high = matrix.astype(ml_dtypes.bfloat16)
    low = (matrix - high.astype(np.float32)).astype(ml_dtypes.bfloat16)
    return np.concatenate([high, high, low], axis=1)


def tables():
    derivative = derivative_table(NP).astype(np.float32).astype(np.float64)
    eye = np.eye(NP)
    inner = three_products(np.kron(eye, derivative))
    inner_t = three_products(np.kron(eye, derivative.T))
    apply_table = np.concatenate([inner, inner_t], axis=0)
    square = derivative * derivative
    diag_table = three_products(np.kron(eye, square.T))
    rows = [[float(v) for v in row] for row in square.T]
    return apply_table, diag_table, rows, [float(v) for v in np.diagonal(derivative)]


def split_rows(values):
    high = values.astype(jnp.bfloat16)
    low = (values - high.astype(jnp.float32)).astype(jnp.bfloat16)
    return jnp.concatenate([high, low, high], axis=0)


def multiply(left, right):
    return jnp.dot(left, right, preferred_element_type=jnp.float32)


def lane_of(rows):
    return lax.broadcasted_iota(jnp.int32, (rows, LANES), 1)


def join_pair(low_face, high_face, lane, unit, number):
    coordinate = (lane // unit) % number
    new_low = low_face + jnp.where(coordinate > 0, pltpu.roll(high_face, unit, 1), 0.0)
    new_high = high_face + jnp.where(
        coordinate < number - 1, pltpu.roll(low_face, LANES - unit, 1), 0.0
    )
    return new_low, new_high


def join_local(ref):
    lane8 = lane_of(8)
    lane64 = lane_of(64)
    for i in range(NP):
        first = slice(i * 64, i * 64 + 8)
        last = slice(i * 64 + 56, i * 64 + 64)
        ref[first, :], ref[last, :] = join_pair(ref[first, :], ref[last, :], lane8, 8, 4)
    ref[0:64, :], ref[448:512, :] = join_pair(ref[0:64, :], ref[448:512, :], lane64, 32, 4)
    first = pl.ds(0, 64, stride=8)
    last = pl.ds(7, 64, stride=8)
    new_first, new_last = join_pair(ref[first, :], ref[last, :], lane64, 1, 8)
    ref[first, :] = new_first
    ref[last, :] = new_last


class Side:
    def __init__(self, sizes, parity):
        a = lax.axis_index("dom")
        b = lax.axis_index("sub")
        last_a = sizes[0] - 1
        last_b = sizes[1] - 1
        self.lr = lax.rem(a + parity, 2)
        self.ls = lax.rem(b + parity, 2)
        self.vr = None
        self.vs = None
        place = 2 * self.lr + self.ls
        dom_step, sub_step = 2, 1
        if parity:
            self.vr = jnp.where(self.lr == 1, a > 0, a < last_a)
            self.vs = jnp.where(self.ls == 1, b > 0, b < last_b)
            row = jnp.logical_or(b == 0, b == last_b)
            column = jnp.logical_or(a == 0, a == last_a)
            rest = jnp.logical_and(a == last_a, b > last_b - 3)
            in_column = ((b + 3) & 3) + jnp.where(rest, 2, 0)
            place = jnp.where(row, (a + 1) & 3, jnp.where(column, in_column, place))
            dom_step = jnp.where(row, 1, 2)
            sub_step = jnp.where(row, 2, 1)
        self.place = place
        self.dom_slot = place ^ dom_step
        self.sub_slot = place ^ sub_step
        self.far_slot = 3 - place
        self.i_row = pl.multiple_of((1 - self.lr) * 448, 64)
        self.j_row = (1 - self.ls) * 56


def keep(mask, *conditions):
    for condition in conditions:
        if condition is not None:
            mask = jnp.logical_and(mask, condition)
    return mask


def pack_faces(ref, side):
    lane = lane_of(16)
    dom_face = jnp.zeros((16, LANES), jnp.float32)
    sub_face = jnp.zeros((16, LANES), jnp.float32)
    for g in range(4):
        block = ref[pl.ds(pl.multiple_of(side.i_row + g * 16, 8), 16), :]
        shift = (g * 32 + 32 * (1 - side.lr)) & 127
        dom_face = jnp.where(lane // 32 == g, pltpu.roll(block, shift, 1), dom_face)
        block = jnp.concatenate(
            [
                ref[pl.ds(pl.multiple_of(i * 64 + side.j_row, 8), 8), :]
                for i in (2 * g, 2 * g + 1)
            ],
            axis=0,
        )
        shift = (g * 8 + 128 - 24 * (1 - side.ls)) & 127
        sub_face = jnp.where((lane // 8) % 4 == g, pltpu.roll(block, shift, 1), sub_face)
    corner = ref[pl.ds(pl.multiple_of(side.i_row + side.j_row, 8), 8), :]
    return dom_face, sub_face, corner


def write_faces(out_ref, field, faces, side):
    dom_face, sub_face, corner = faces
    row = field * 16
    out_ref[side.dom_slot, row : row + 16, :] = dom_face
    out_ref[side.sub_slot, row : row + 16, :] = sub_face
    out_ref[side.far_slot, row : row + 8, :] = corner
    out_ref[side.far_slot, row + 8 : row + 16, :] = jnp.zeros((8, LANES), jnp.float32)
    out_ref[side.place, row : row + 16, :] = jnp.zeros((16, LANES), jnp.float32)


def add_faces(ref, recv_ref, field, side):
    lane = lane_of(16)
    lane8 = lane_of(8)
    row = field * 16
    dom_face = recv_ref[side.dom_slot, row : row + 16, :]
    for g in range(4):
        shift = (96 * (1 - side.lr) + 128 - g * 32) & 127
        mask = keep(lane // 32 == 3 * (1 - side.lr), side.vr)
        at = pl.ds(pl.multiple_of(side.i_row + g * 16, 8), 16)
        ref[at, :] = ref[at, :] + jnp.where(mask, pltpu.roll(dom_face, shift, 1), 0.0)
    sub_mask = keep((lane8 // 8) % 4 == 3 * (1 - side.ls), side.vs)
    sub_face = recv_ref[side.sub_slot, row : row + 16, :]
    for g in range(4):
        shift = (24 * (1 - side.ls) + 128 - g * 8) & 127
        rolled = pltpu.roll(sub_face, shift, 1)
        for part in range(2):
            at = pl.ds(pl.multiple_of((2 * g + part) * 64 + side.j_row, 8), 8)
            piece = rolled[part * 8 : part * 8 + 8, :]
            ref[at, :] = ref[at, :] + jnp.where(sub_mask, piece, 0.0)
    corner = recv_ref[side.far_slot, row : row + 8, :]
    offset = 96 * (1 - side.lr) + 24 * (1 - side.ls)
    shift = (2 * offset + 256 - 120) & 127
    mask = keep(lane8 // 8 == offset // 8, side.vr, side.vs)
    at = pl.ds(pl.multiple_of(side.i_row + side.j_row, 8), 8)
    ref[at, :] = ref[at, :] + jnp.where(mask, pltpu.roll(corner, shift, 1), 0.0)


def halves(matrix):
    flipped = matrix[:, ::-1]
    even = 0.5 * (matrix + flipped)[:4, :4]
    odd = 0.5 * (matrix - flipped)[:4, :4]
    return [[float(v) for v in row] for row in even], [[float(v) for v in row] for row in odd]


def blend(parts, matrix):
    out = []
    for row in matrix:
        total = parts[0] * row[0]
        for a in range(1, NP):
            total = total + parts[a] * row[a]
        out.append(total)
    return out


def derive(parts, pair):
    even, odd = pair
    sums = [parts[a] + parts[7 - a] for a in range(4)]
    gaps = [parts[a] - parts[7 - a] for a in range(4)]
    low = []
    high = []
    for i in range(4):
        first = sums[0] * even[i][0]
        second = gaps[0] * odd[i][0]
        for a in range(1, 4):
            first = first + sums[a] * even[i][a]
            second = second + gaps[a] * odd[i][a]
        low.append(second + first)
        high.append(second - first)
    return low + high[::-1]


def apply_operator(value_ref, geo_ref, table_ref, image_ref, work_ref):
    forward, backward = PAIRS
    inner = table_ref[0:64, :]
    inner_t = table_ref[64:128, :]
    for j in range(NP):
        rows = [slice(i * 64 + j * 8, i * 64 + j * 8 + 8) for i in range(NP)]
        for at, part in zip(rows, derive([value_ref[at, :] for at in rows], forward)):
            work_ref[at, :] = part
    for i in range(NP):
        at = slice(i * 64, i * 64 + 64)
        rows = [slice(i * 64 + j * 8, i * 64 + j * 8 + 8) for j in range(NP)]
        grad_t = multiply(inner, split_rows(value_ref[at, :]))
        grad_r = work_ref[at, :]
        grad_s = jnp.concatenate(derive([value_ref[row, :] for row in rows], forward), axis=0)
        g = [geo_ref[index, at, :].astype(jnp.float32) for index in range(6)]
        work_ref[at, :] = g[0] * grad_r + g[3] * grad_s + g[4] * grad_t
        flux_s = g[3] * grad_r + g[1] * grad_s + g[5] * grad_t
        flux_t = g[4] * grad_r + g[5] * grad_s + g[2] * grad_t
        from_s = derive([flux_s[j * 8 : j * 8 + 8, :] for j in range(NP)], backward)
        image_ref[at, :] = jnp.concatenate(from_s, axis=0) + multiply(
            inner_t, split_rows(flux_t)
        )
    for j in range(NP):
        rows = [slice(i * 64 + j * 8, i * 64 + j * 8 + 8) for i in range(NP)]
        for at, part in zip(rows, derive([work_ref[at, :] for at in rows], backward)):
            image_ref[at, :] = image_ref[at, :] + part


PAIRS = tuple(
    halves(m) for m in (derivative_table(NP).astype(np.float32), derivative_table(NP).T.astype(np.float32))
)


def emit_faces(ref, field, send_ref, later_ref, sides):
    write_faces(send_ref, field, pack_faces(ref, sides[0]), sides[0])
    write_faces(later_ref, field, pack_faces(ref, sides[1]), sides[1])


def permute_exact(values, table):
    total = None
    for part in range(3):
        piece = values.astype(jnp.bfloat16)
        moved = multiply(piece, table)
        values = values - piece.astype(jnp.float32)
        total = moved if total is None else total + moved
    return total


def begin_kernel(sizes, order, square, middle, geo_hbm, load_hbm, cells_hbm, table_hbm, geo_out, parts_ref, one_hot_ref, send_ref, later_ref, work_ref, geo_ref, load_ref, cells_ref, table_ref, sems):
    copies = [pltpu.make_async_copy(cells_hbm, cells_ref, sems.at[0])]
    for index in range(6):
        copies.append(
            pltpu.make_async_copy(geo_hbm.at[index], geo_ref.at[index], sems.at[1 + index])
        )
    copies.append(pltpu.make_async_copy(table_hbm, table_ref, sems.at[7]))
    copies.append(pltpu.make_async_copy(load_hbm, load_ref, sems.at[8]))
    for copy in copies:
        copy.start()
    copies[0].wait()
    cell = lax.broadcasted_iota(jnp.int32, (LANES, LANES), 0)
    by_cell = jnp.where(cell == jnp.broadcast_to(cells_ref[...], (LANES, LANES)), 1.0, 0.0)
    one_hot_ref[...] = by_cell.astype(jnp.bfloat16)
    table = by_cell.T.astype(jnp.bfloat16)
    load_part = parts_ref.at[0]
    diag_part = parts_ref.at[1]
    copies[1].wait()
    first = multiply(geo_ref[0], table)
    geo_out[0] = first.astype(jnp.bfloat16)
    work_ref[...] = first
    for index in range(1, 6):
        copies[1 + index].wait()
        geo_out[index] = multiply(geo_ref[index], table).astype(jnp.bfloat16)
    copies[7].wait()
    inner = table_ref[...]
    for j in range(NP):
        rows = [slice(i * 64 + j * 8, i * 64 + j * 8 + 8) for i in range(NP)]
        for at, part in zip(rows, blend([work_ref[at, :] for at in rows], square)):
            diag_part[at, :] = part
    copies[8].wait()
    sub_row = lax.broadcasted_iota(jnp.int32, (64, LANES), 0) % 8
    third = jnp.where(sub_row == 0, middle[0], jnp.where(sub_row == 7, middle[7], 0.0))
    for i in range(NP):
        at = slice(i * 64, i * 64 + 64)
        load_part[at, :] = permute_exact(load_ref[at, :], table)
        second = geo_out[1, at, :].astype(jnp.float32)
        fifth = geo_out[5, at, :].astype(jnp.float32)
        pieces = blend([second[j * 8 : j * 8 + 8, :] for j in range(NP)], square)
        for j in (0, 7):
            extra = middle[j] * third[0:8, :] * fifth[j * 8 : j * 8 + 8, :]
            if i in (0, 7):
                cross = geo_out[3, at, :].astype(jnp.float32)[j * 8 : j * 8 + 8, :]
                extra = extra + middle[i] * middle[j] * cross
            pieces[j] = pieces[j] + 2.0 * extra
        total = jnp.concatenate(pieces, axis=0)
        total = total + multiply(inner, split_rows(geo_out[2, at, :].astype(jnp.float32)))
        if i in (0, 7):
            total = total + 2.0 * middle[i] * third * geo_out[4, at, :].astype(jnp.float32)
        diag_part[at, :] = diag_part[at, :] + total
    sides = two_sides(sizes, order)
    for field in range(2):
        join_local(parts_ref.at[field])
        emit_faces(parts_ref.at[field], field, send_ref, later_ref, sides)


def middle_kernel(sizes, order, fields, recv_ref, later_ref, out_ref):
    now, then = two_sides(sizes, order)
    out_ref[...] = later_ref[...]
    lane = lane_of(8)
    for field in range(fields):
        row = field * 16

        def correct(slot_in, low_in, slot_out, low_out, valid):
            piece = recv_ref[slot_in, pl.ds(pl.multiple_of(row + 8 * (1 - low_in), 8), 8), :]
            shift = (8 + 128 - 8 * (1 - low_out) + 8 * (1 - low_in) - 8) & 127
            mask = keep(lane // 8 == 15 * (1 - low_out), valid)
            at = pl.ds(pl.multiple_of(row + 8 * (1 - low_out), 8), 8)
            out_ref[slot_out, at, :] = out_ref[slot_out, at, :] + jnp.where(
                mask, pltpu.roll(piece, shift, 1), 0.0
            )

        correct(now.sub_slot, then.lr, then.dom_slot, now.ls, now.vs)
        correct(now.dom_slot, then.ls, then.sub_slot, now.lr, now.vr)


def two_sides(sizes, order):
    return Side(sizes, order[0]), Side(sizes, order[1])


def coefficients():
    centre = 0.5 * (cheb_high + cheb_low)
    half_width = 0.5 * (cheb_high - cheb_low)
    ratio = centre / half_width
    rho_now = 1.0 / ratio
    steps = []
    for step in range(APPLY):
        rho_new = 1.0 / (2.0 * ratio - rho_now)
        steps.append((rho_new * rho_now, 2.0 * rho_new / half_width))
        rho_now = rho_new
    return centre, steps


def first_kernel(sizes, before, order, centre, parts_ref, recv_ref, recv2_ref, geo_ref, table_ref, residual_ref, diag_ref, direction_ref, image_ref, send_ref, later_ref, work_ref):
    sides = two_sides(sizes, before)
    residual_ref[...] = parts_ref[0]
    diag_ref[...] = parts_ref[1]
    for field, ref in ((0, residual_ref), (1, diag_ref)):
        add_faces(ref, recv_ref, field, sides[0])
        add_faces(ref, recv2_ref, field, sides[1])
    direction_ref[...] = residual_ref[...] / diag_ref[...] / centre
    apply_operator(direction_ref, geo_ref, table_ref, image_ref, work_ref)
    join_local(image_ref)
    emit_faces(image_ref, 0, send_ref, later_ref, two_sides(sizes, order))


def step_kernel(sizes, before, order, pair, part_ref, recv_ref, recv2_ref, geo_ref, table_ref, old_residual_ref, diag_ref, old_direction_ref, residual_ref, direction_ref, image_ref, send_ref, later_ref, work_ref):
    sides = two_sides(sizes, before)
    work_ref[...] = part_ref[...]
    add_faces(work_ref, recv_ref, 0, sides[0])
    add_faces(work_ref, recv2_ref, 0, sides[1])
    residual = old_residual_ref[...] - work_ref[...]
    residual_ref[...] = residual
    direction_ref[...] = pair[0] * old_direction_ref[...] + pair[1] * (residual / diag_ref[...])
    apply_operator(direction_ref, geo_ref, table_ref, image_ref, work_ref)
    join_local(image_ref)
    emit_faces(image_ref, 0, send_ref, later_ref, two_sides(sizes, order))


def end_kernel(sizes, before, pair, part_ref, recv_ref, recv2_ref, residual_ref, diag_ref, d0_ref, d1_ref, d2_ref, d3_ref, one_hot_ref, out_hbm, work_ref, out_ref, sems):
    sides = two_sides(sizes, before)
    work_ref[...] = part_ref[...]
    add_faces(work_ref, recv_ref, 0, sides[0])
    add_faces(work_ref, recv2_ref, 0, sides[1])
    table = one_hot_ref[...]
    copies = []
    for i in range(NP):
        at = slice(i * 64, i * 64 + 64)
        residual = residual_ref[at, :] - work_ref[at, :]
        last = d3_ref[at, :]
        direction = pair[0] * last + pair[1] * (residual / diag_ref[at, :])
        iterate = d0_ref[at, :] + d1_ref[at, :] + d2_ref[at, :] + last + direction
        out_ref[at, :] = permute_exact(iterate, table)
        if i % 2 == 1:
            here = pl.ds((i - 1) * 64, 128)
            copy = pltpu.make_async_copy(out_ref.at[here], out_hbm.at[here], sems.at[i // 2])
            copy.start()
            copies.append(copy)
    for copy in copies:
        copy.wait()


def call(kernel, outs, *operands, scratch=(), name=None, **specs):
    return pl.pallas_call(
        kernel,
        out_shape=outs,
        scratch_shapes=list(scratch),
        compiler_params=pltpu.CompilerParams(vmem_limit_bytes=32 * 2**20),
        name=name,
        **specs,
    )(*operands)


def exchange_groups(sizes, parity):
    dom, sub = sizes
    whole = []
    if parity:
        for b in (0, sub - 1):
            whole += [[((a + step) % dom, b) for step in range(4)] for a in range(-1, dom - 1, 4)]
        full = 4 * ((sub - 2) // 4)
        for a in (0, dom - 1):
            whole += [[(a, b + step) for step in range(4)] for b in range(1, 1 + full, 4)]
        whole.append([(a, b) for a in (0, dom - 1) for b in (sub - 3, sub - 2)])
    for a in range(parity, dom - 1, 2):
        for b in range(parity, sub - 1, 2):
            whole.append([(a + da, b + db) for da in (0, 1) for db in (0, 1)])
    return [[a * sub + b for a, b in group] for group in whole]


def solution(mesh):
    sizes = (mesh.shape["dom"], mesh.shape["sub"])
    apply_table, diag_table, square, middle = tables()
    centre, steps = coefficients()
    field = jax.ShapeDtypeStruct((ROWS, LANES), jnp.float32)
    one = jax.ShapeDtypeStruct((4, 16, LANES), jnp.float32)
    two = jax.ShapeDtypeStruct((4, 32, LANES), jnp.float32)

    work = pltpu.VMEM((ROWS, LANES), jnp.float32)
    far = pl.BlockSpec(memory_space=pltpu.HBM)
    near = pl.BlockSpec(memory_space=pltpu.VMEM)
    orders = ORDERS

    def exchange(send, parity):
        return lax.all_to_all(
            send,
            ("dom", "sub"),
            0,
            0,
            axis_index_groups=exchange_groups(sizes, parity),
            tiled=True,
        )

    def assemble(send, later, order, fields):
        shape = one if fields == 1 else two
        recv = exchange(send, order[0])
        send2 = call(
            functools.partial(middle_kernel, sizes, order, fields), shape, recv, later, name="faces"
        )
        return recv, exchange(send2, order[1])

    def shards(geometry, load, cells):
        table = jnp.asarray(apply_table)
        geo, parts, one_hot, send, later = call(
            functools.partial(begin_kernel, sizes, orders[0], square, middle),
            (
                jax.ShapeDtypeStruct(geometry.shape, jnp.bfloat16),
                jax.ShapeDtypeStruct((2, ROWS, LANES), jnp.float32),
                jax.ShapeDtypeStruct((LANES, LANES), jnp.bfloat16),
                two,
                two,
            ),
            *[
                pltpu.with_memory_space_constraint(array, pltpu.HBM)
                for array in (geometry, load, cells, jnp.asarray(diag_table))
            ],
            in_specs=[far] * 4,
            scratch=(
                work,
                pltpu.VMEM(geometry.shape, jnp.bfloat16),
                work,
                pltpu.VMEM(cells.shape, jnp.int32),
                pltpu.VMEM(diag_table.shape, jnp.bfloat16),
                pltpu.SemaphoreType.DMA((9,)),
            ),
            name="begin",
        )
        recv, recv2 = assemble(send, later, orders[0], 2)
        residual, diag, direction, image, send, later = call(
            functools.partial(first_kernel, sizes, orders[0], orders[1], centre),
            (field, field, field, field, one, one),
            parts,
            recv,
            recv2,
            geo,
            table,
            scratch=(work,),
            name="first",
        )
        directions = [direction]
        for step, pair in enumerate(steps[:-1]):
            recv, recv2 = assemble(send, later, orders[step + 1], 1)
            residual, direction, image, send, later = call(
                functools.partial(step_kernel, sizes, orders[step + 1], orders[step + 2], pair),
                (field, field, field, one, one),
                image,
                recv,
                recv2,
                geo,
                table,
                residual,
                diag,
                direction,
                scratch=(work,),
                name="step",
            )
            directions.append(direction)
        recv, recv2 = assemble(send, later, orders[APPLY], 1)
        return call(
            functools.partial(end_kernel, sizes, orders[APPLY], steps[-1]),
            field,
            image,
            recv,
            recv2,
            residual,
            diag,
            *directions,
            one_hot,
            in_specs=[near] * 10,
            out_specs=far,
            scratch=(work, work, pltpu.SemaphoreType.DMA((4,))),
            name="end",
        )

    placed = (P(None, None, ("dom", "sub")), P(None, ("dom", "sub")), P(("dom", "sub"), None))
    return jax.shard_map(
        shards, mesh=mesh, in_specs=placed, out_specs=P(None, ("dom", "sub")), check_vma=False
    )
```

```python
import functools

import jax
import jax.numpy as jnp
import ml_dtypes
import numpy as np
from jax import lax
from jax.experimental import pallas as pl
from jax.experimental.pallas import tpu as pltpu
from jax.sharding import PartitionSpec as P

NP = 8
APPLY = 4
ORDERS = ((0, 1), (1, 0), (0, 1), (1, 0), (0, 1))
LANES = 128
ROWS = NP**3

cheb_low = 0.4
cheb_high = 4.0


def legendre_values(points, degree):
    before = np.ones(points.shape[0])
    current = points.copy()
    for order in range(2, degree + 1):
        following = ((2 * order - 1) * points * current - (order - 1) * before) / order
        before = current
        current = following
    return (current, before)


def derivative_table(number):
    degree = number - 1
    points = np.cos(np.pi * np.arange(degree + 1) / degree)
    for sweep in range(60):
        current, before = legendre_values(points, degree)
        inner = points[1:-1]
        step_size = (inner * current[1:-1] - before[1:-1]) / ((degree + 1) * current[1:-1])
        points = np.concatenate([points[:1], inner - step_size, points[-1:]])
    points = np.sort(points)
    points = np.concatenate([np.zeros(1) - 1.0, points[1:-1], np.zeros(1) + 1.0])
    values, unused = legendre_values(points, degree)
    matrix = np.zeros((number, number))
    for row_index in range(number):
        for col_index in range(number):
            if row_index != col_index:
                matrix[row_index, col_index] = values[row_index] / (
                    values[col_index] * (points[row_index] - points[col_index])
                )
    matrix[0, 0] = -degree * (degree + 1) / 4.0
    matrix[degree, degree] = degree * (degree + 1) / 4.0
    return matrix


def three_products(matrix):
    matrix = matrix.astype(np.float32)
    high = matrix.astype(ml_dtypes.bfloat16)
    low = (matrix - high.astype(np.float32)).astype(ml_dtypes.bfloat16)
    return np.concatenate([high, high, low], axis=1)


def tables():
    derivative = derivative_table(NP).astype(np.float32).astype(np.float64)
    eye = np.eye(NP)
    inner = three_products(np.kron(eye, derivative))
    inner_t = three_products(np.kron(eye, derivative.T))
    apply_table = np.concatenate([inner, inner_t], axis=0)
    square = derivative * derivative
    diag_table = three_products(np.kron(eye, square.T))
    rows = [[float(v) for v in row] for row in square.T]
    return apply_table, diag_table, rows, [float(v) for v in np.diagonal(derivative)]


def split_rows(values):
    high = values.astype(jnp.bfloat16)
    low = (values - high.astype(jnp.float32)).astype(jnp.bfloat16)
    return jnp.concatenate([high, low, high], axis=0)


def multiply(left, right):
    return jnp.dot(left, right, preferred_element_type=jnp.float32)


def lane_of(rows):
    return lax.broadcasted_iota(jnp.int32, (rows, LANES), 1)


def join_pair(low_face, high_face, lane, unit, number):
    coordinate = (lane // unit) % number
    new_low = low_face + jnp.where(coordinate > 0, pltpu.roll(high_face, unit, 1), 0.0)
    new_high = high_face + jnp.where(
        coordinate < number - 1, pltpu.roll(low_face, LANES - unit, 1), 0.0
    )
    return new_low, new_high


def join_local(ref):
    lane8 = lane_of(8)
    lane64 = lane_of(64)
    for i in range(NP):
        first = slice(i * 64, i * 64 + 8)
        last = slice(i * 64 + 56, i * 64 + 64)
        ref[first, :], ref[last, :] = join_pair(ref[first, :], ref[last, :], lane8, 8, 4)
    ref[0:64, :], ref[448:512, :] = join_pair(ref[0:64, :], ref[448:512, :], lane64, 32, 4)
    first = pl.ds(0, 64, stride=8)
    last = pl.ds(7, 64, stride=8)
    new_first, new_last = join_pair(ref[first, :], ref[last, :], lane64, 1, 8)
    ref[first, :] = new_first
    ref[last, :] = new_last


class Side:
    def __init__(self, sizes, parity):
        a = lax.axis_index("dom")
        b = lax.axis_index("sub")
        last_a = sizes[0] - 1
        last_b = sizes[1] - 1
        self.lr = lax.rem(a + parity, 2)
        self.ls = lax.rem(b + parity, 2)
        self.vr = None
        self.vs = None
        place = 2 * self.lr + self.ls
        dom_step, sub_step = 2, 1
        if parity:
            self.vr = jnp.where(self.lr == 1, a > 0, a < last_a)
            self.vs = jnp.where(self.ls == 1, b > 0, b < last_b)
            row = jnp.logical_or(b == 0, b == last_b)
            column = jnp.logical_or(a == 0, a == last_a)
            rest = jnp.logical_and(a == last_a, b > last_b - 3)
            in_column = ((b + 3) & 3) + jnp.where(rest, 2, 0)
            place = jnp.where(row, (a + 1) & 3, jnp.where(column, in_column, place))
            dom_step = jnp.where(row, 1, 2)
            sub_step = jnp.where(row, 2, 1)
        self.place = place
        self.dom_slot = place ^ dom_step
        self.sub_slot = place ^ sub_step
        self.far_slot = 3 - place
        self.i_row = pl.multiple_of((1 - self.lr) * 448, 64)
        self.j_row = (1 - self.ls) * 56


def keep(mask, *conditions):
    for condition in conditions:
        if condition is not None:
            mask = jnp.logical_and(mask, condition)
    return mask


def pack_faces(ref, side):
    lane = lane_of(16)
    dom_face = jnp.zeros((16, LANES), jnp.float32)
    sub_face = jnp.zeros((16, LANES), jnp.float32)
    for g in range(4):
        block = ref[pl.ds(pl.multiple_of(side.i_row + g * 16, 8), 16), :]
        shift = (g * 32 + 32 * (1 - side.lr)) & 127
        dom_face = jnp.where(lane // 32 == g, pltpu.roll(block, shift, 1), dom_face)
        block = jnp.concatenate(
            [
                ref[pl.ds(pl.multiple_of(i * 64 + side.j_row, 8), 8), :]
                for i in (2 * g, 2 * g + 1)
            ],
            axis=0,
        )
        shift = (g * 8 + 128 - 24 * (1 - side.ls)) & 127
        sub_face = jnp.where((lane // 8) % 4 == g, pltpu.roll(block, shift, 1), sub_face)
    corner = ref[pl.ds(pl.multiple_of(side.i_row + side.j_row, 8), 8), :]
    return dom_face, sub_face, corner


def write_faces(out_ref, field, faces, side):
    dom_face, sub_face, corner = faces
    row = field * 16
    out_ref[side.dom_slot, row : row + 16, :] = dom_face
    out_ref[side.sub_slot, row : row + 16, :] = sub_face
    out_ref[side.far_slot, row : row + 8, :] = corner
    out_ref[side.far_slot, row + 8 : row + 16, :] = jnp.zeros((8, LANES), jnp.float32)
    out_ref[side.place, row : row + 16, :] = jnp.zeros((16, LANES), jnp.float32)


def add_faces(ref, recv_ref, field, side):
    lane = lane_of(16)
    lane8 = lane_of(8)
    row = field * 16
    dom_face = recv_ref[side.dom_slot, row : row + 16, :]
    for g in range(4):
        shift = (96 * (1 - side.lr) + 128 - g * 32) & 127
        mask = keep(lane // 32 == 3 * (1 - side.lr), side.vr)
        at = pl.ds(pl.multiple_of(side.i_row + g * 16, 8), 16)
        ref[at, :] = ref[at, :] + jnp.where(mask, pltpu.roll(dom_face, shift, 1), 0.0)
    sub_mask = keep((lane8 // 8) % 4 == 3 * (1 - side.ls), side.vs)
    sub_face = recv_ref[side.sub_slot, row : row + 16, :]
    for g in range(4):
        shift = (24 * (1 - side.ls) + 128 - g * 8) & 127
        rolled = pltpu.roll(sub_face, shift, 1)
        for part in range(2):
            at = pl.ds(pl.multiple_of((2 * g + part) * 64 + side.j_row, 8), 8)
            piece = rolled[part * 8 : part * 8 + 8, :]
            ref[at, :] = ref[at, :] + jnp.where(sub_mask, piece, 0.0)
    corner = recv_ref[side.far_slot, row : row + 8, :]
    offset = 96 * (1 - side.lr) + 24 * (1 - side.ls)
    shift = (2 * offset + 256 - 120) & 127
    mask = keep(lane8 // 8 == offset // 8, side.vr, side.vs)
    at = pl.ds(pl.multiple_of(side.i_row + side.j_row, 8), 8)
    ref[at, :] = ref[at, :] + jnp.where(mask, pltpu.roll(corner, shift, 1), 0.0)


def halves(matrix):
    flipped = matrix[:, ::-1]
    even = 0.5 * (matrix + flipped)[:4, :4]
    odd = 0.5 * (matrix - flipped)[:4, :4]
    return [[float(v) for v in row] for row in even], [[float(v) for v in row] for row in odd]


def blend(parts, matrix):
    out = []
    for row in matrix:
        total = parts[0] * row[0]
        for a in range(1, NP):
            total = total + parts[a] * row[a]
        out.append(total)
    return out


def derive(parts, pair):
    even, odd = pair
    sums = [parts[a] + parts[7 - a] for a in range(4)]
    gaps = [parts[a] - parts[7 - a] for a in range(4)]
    low = []
    high = []
    for i in range(4):
        first = sums[0] * even[i][0]
        second = gaps[0] * odd[i][0]
        for a in range(1, 4):
            first = first + sums[a] * even[i][a]
            second = second + gaps[a] * odd[i][a]
        low.append(second + first)
        high.append(second - first)
    return low + high[::-1]


def apply_operator(value_ref, geo_ref, table_ref, image_ref, work_ref):
    forward, backward = PAIRS
    inner = table_ref[0:64, :]
    inner_t = table_ref[64:128, :]
    for j in range(NP):
        rows = [slice(i * 64 + j * 8, i * 64 + j * 8 + 8) for i in range(NP)]
        for at, part in zip(rows, derive([value_ref[at, :] for at in rows], forward)):
            work_ref[at, :] = part
    for i in range(NP):
        at = slice(i * 64, i * 64 + 64)
        rows = [slice(i * 64 + j * 8, i * 64 + j * 8 + 8) for j in range(NP)]
        grad_t = multiply(inner, split_rows(value_ref[at, :]))
        grad_r = work_ref[at, :]
        grad_s = jnp.concatenate(derive([value_ref[row, :] for row in rows], forward), axis=0)
        g = [geo_ref[index, at, :].astype(jnp.float32) for index in range(6)]
        work_ref[at, :] = g[0] * grad_r + g[3] * grad_s + g[4] * grad_t
        flux_s = g[3] * grad_r + g[1] * grad_s + g[5] * grad_t
        flux_t = g[4] * grad_r + g[5] * grad_s + g[2] * grad_t
        from_s = derive([flux_s[j * 8 : j * 8 + 8, :] for j in range(NP)], backward)
        image_ref[at, :] = jnp.concatenate(from_s, axis=0) + multiply(
            inner_t, split_rows(flux_t)
        )
    for j in range(NP):
        rows = [slice(i * 64 + j * 8, i * 64 + j * 8 + 8) for i in range(NP)]
        for at, part in zip(rows, derive([work_ref[at, :] for at in rows], backward)):
            image_ref[at, :] = image_ref[at, :] + part


PAIRS = tuple(
    halves(m) for m in (derivative_table(NP).astype(np.float32), derivative_table(NP).T.astype(np.float32))
)


def emit_faces(ref, field, send_ref, later_ref, sides):
    write_faces(send_ref, field, pack_faces(ref, sides[0]), sides[0])
    write_faces(later_ref, field, pack_faces(ref, sides[1]), sides[1])


def permute_exact(values, table):
    total = None
    for part in range(3):
        piece = values.astype(jnp.bfloat16)
        moved = multiply(piece, table)
        values = values - piece.astype(jnp.float32)
        total = moved if total is None else total + moved
    return total


def begin_kernel(sizes, order, square, middle, geo_hbm, load_hbm, cells_hbm, table_hbm, geo_out, parts_ref, one_hot_ref, send_ref, later_ref, work_ref, geo_ref, load_ref, cells_ref, table_ref, sems):
    copies = [
        pltpu.make_async_copy(source, target, sems.at[index])
        for index, (source, target) in enumerate(
            (
                (cells_hbm, cells_ref),
                (geo_hbm, geo_ref),
                (load_hbm, load_ref),
                (table_hbm, table_ref),
            )
        )
    ]
    for copy in copies:
        copy.start()
    copies[0].wait()
    cell = lax.broadcasted_iota(jnp.int32, (LANES, LANES), 0)
    by_cell = jnp.where(cell == jnp.broadcast_to(cells_ref[...], (LANES, LANES)), 1.0, 0.0)
    one_hot_ref[...] = by_cell.astype(jnp.bfloat16)
    table = by_cell.T.astype(jnp.bfloat16)
    load_part = parts_ref.at[0]
    diag_part = parts_ref.at[1]
    for copy in copies[1:]:
        copy.wait()
    for index in range(6):
        moved = multiply(geo_ref[index], table)
        geo_out[index] = moved.astype(jnp.bfloat16)
        if index == 0:
            work_ref[...] = moved
    inner = table_ref[...]
    for j in range(NP):
        rows = [slice(i * 64 + j * 8, i * 64 + j * 8 + 8) for i in range(NP)]
        for at, part in zip(rows, blend([work_ref[at, :] for at in rows], square)):
            diag_part[at, :] = part
    sub_row = lax.broadcasted_iota(jnp.int32, (64, LANES), 0) % 8
    third = jnp.where(sub_row == 0, middle[0], jnp.where(sub_row == 7, middle[7], 0.0))
    for i in range(NP):
        at = slice(i * 64, i * 64 + 64)
        load_part[at, :] = permute_exact(load_ref[at, :], table)
        second = geo_out[1, at, :].astype(jnp.float32)
        fifth = geo_out[5, at, :].astype(jnp.float32)
        pieces = blend([second[j * 8 : j * 8 + 8, :] for j in range(NP)], square)
        for j in (0, 7):
            extra = middle[j] * third[0:8, :] * fifth[j * 8 : j * 8 + 8, :]
            if i in (0, 7):
                cross = geo_out[3, at, :].astype(jnp.float32)[j * 8 : j * 8 + 8, :]
                extra = extra + middle[i] * middle[j] * cross
            pieces[j] = pieces[j] + 2.0 * extra
        total = jnp.concatenate(pieces, axis=0)
        total = total + multiply(inner, split_rows(geo_out[2, at, :].astype(jnp.float32)))
        if i in (0, 7):
            total = total + 2.0 * middle[i] * third * geo_out[4, at, :].astype(jnp.float32)
        diag_part[at, :] = diag_part[at, :] + total
    sides = two_sides(sizes, order)
    for field in range(2):
        join_local(parts_ref.at[field])
        emit_faces(parts_ref.at[field], field, send_ref, later_ref, sides)


def middle_kernel(sizes, order, fields, recv_ref, later_ref, out_ref):
    now, then = two_sides(sizes, order)
    out_ref[...] = later_ref[...]
    lane = lane_of(8)
    for field in range(fields):
        row = field * 16

        def correct(slot_in, low_in, slot_out, low_out, valid):
            piece = recv_ref[slot_in, pl.ds(pl.multiple_of(row + 8 * (1 - low_in), 8), 8), :]
            shift = (8 + 128 - 8 * (1 - low_out) + 8 * (1 - low_in) - 8) & 127
            mask = keep(lane // 8 == 15 * (1 - low_out), valid)
            at = pl.ds(pl.multiple_of(row + 8 * (1 - low_out), 8), 8)
            out_ref[slot_out, at, :] = out_ref[slot_out, at, :] + jnp.where(
                mask, pltpu.roll(piece, shift, 1), 0.0
            )

        correct(now.sub_slot, then.lr, then.dom_slot, now.ls, now.vs)
        correct(now.dom_slot, then.ls, then.sub_slot, now.lr, now.vr)


def two_sides(sizes, order):
    return Side(sizes, order[0]), Side(sizes, order[1])


def coefficients():
    centre = 0.5 * (cheb_high + cheb_low)
    half_width = 0.5 * (cheb_high - cheb_low)
    ratio = centre / half_width
    rho_now = 1.0 / ratio
    steps = []
    for step in range(APPLY):
        rho_new = 1.0 / (2.0 * ratio - rho_now)
        steps.append((rho_new * rho_now, 2.0 * rho_new / half_width))
        rho_now = rho_new
    return centre, steps


def first_kernel(sizes, before, order, centre, parts_ref, recv_ref, recv2_ref, geo_ref, table_ref, residual_ref, diag_ref, direction_ref, image_ref, send_ref, later_ref, work_ref):
    sides = two_sides(sizes, before)
    residual_ref[...] = parts_ref[0]
    diag_ref[...] = parts_ref[1]
    for field, ref in ((0, residual_ref), (1, diag_ref)):
        add_faces(ref, recv_ref, field, sides[0])
        add_faces(ref, recv2_ref, field, sides[1])
    direction_ref[...] = residual_ref[...] / diag_ref[...] / centre
    apply_operator(direction_ref, geo_ref, table_ref, image_ref, work_ref)
    join_local(image_ref)
    emit_faces(image_ref, 0, send_ref, later_ref, two_sides(sizes, order))


def step_kernel(sizes, before, order, pair, part_ref, recv_ref, recv2_ref, geo_ref, table_ref, old_residual_ref, diag_ref, old_direction_ref, residual_ref, direction_ref, image_ref, send_ref, later_ref, work_ref):
    sides = two_sides(sizes, before)
    work_ref[...] = part_ref[...]
    add_faces(work_ref, recv_ref, 0, sides[0])
    add_faces(work_ref, recv2_ref, 0, sides[1])
    residual = old_residual_ref[...] - work_ref[...]
    residual_ref[...] = residual
    direction_ref[...] = pair[0] * old_direction_ref[...] + pair[1] * (residual / diag_ref[...])
    apply_operator(direction_ref, geo_ref, table_ref, image_ref, work_ref)
    join_local(image_ref)
    emit_faces(image_ref, 0, send_ref, later_ref, two_sides(sizes, order))


def end_kernel(sizes, before, pair, part_ref, recv_ref, recv2_ref, residual_ref, diag_ref, d0_ref, d1_ref, d2_ref, d3_ref, one_hot_ref, out_hbm, work_ref, out_ref, sems):
    sides = two_sides(sizes, before)
    work_ref[...] = part_ref[...]
    add_faces(work_ref, recv_ref, 0, sides[0])
    add_faces(work_ref, recv2_ref, 0, sides[1])
    table = one_hot_ref[...]
    copies = []
    for i in range(NP):
        at = slice(i * 64, i * 64 + 64)
        residual = residual_ref[at, :] - work_ref[at, :]
        last = d3_ref[at, :]
        direction = pair[0] * last + pair[1] * (residual / diag_ref[at, :])
        iterate = d0_ref[at, :] + d1_ref[at, :] + d2_ref[at, :] + last + direction
        out_ref[at, :] = permute_exact(iterate, table)
        if i % 2 == 1:
            here = pl.ds((i - 1) * 64, 128)
            copy = pltpu.make_async_copy(out_ref.at[here], out_hbm.at[here], sems.at[i // 2])
            copy.start()
            copies.append(copy)
    for copy in copies:
        copy.wait()


def call(kernel, outs, *operands, scratch=(), name=None, **specs):
    return pl.pallas_call(
        kernel,
        out_shape=outs,
        scratch_shapes=list(scratch),
        compiler_params=pltpu.CompilerParams(vmem_limit_bytes=32 * 2**20),
        name=name,
        **specs,
    )(*operands)


def exchange_groups(sizes, parity):
    dom, sub = sizes
    whole = []
    if parity:
        for b in (0, sub - 1):
            whole += [[((a + step) % dom, b) for step in range(4)] for a in range(-1, dom - 1, 4)]
        full = 4 * ((sub - 2) // 4)
        for a in (0, dom - 1):
            whole += [[(a, b + step) for step in range(4)] for b in range(1, 1 + full, 4)]
        whole.append([(a, b) for a in (0, dom - 1) for b in (sub - 3, sub - 2)])
    for a in range(parity, dom - 1, 2):
        for b in range(parity, sub - 1, 2):
            whole.append([(a + da, b + db) for da in (0, 1) for db in (0, 1)])
    return [[a * sub + b for a, b in group] for group in whole]


def solution(mesh):
    sizes = (mesh.shape["dom"], mesh.shape["sub"])
    apply_table, diag_table, square, middle = tables()
    centre, steps = coefficients()
    field = jax.ShapeDtypeStruct((ROWS, LANES), jnp.float32)
    one = jax.ShapeDtypeStruct((4, 16, LANES), jnp.float32)
    two = jax.ShapeDtypeStruct((4, 32, LANES), jnp.float32)

    work = pltpu.VMEM((ROWS, LANES), jnp.float32)
    far = pl.BlockSpec(memory_space=pltpu.HBM)
    near = pl.BlockSpec(memory_space=pltpu.VMEM)
    orders = ORDERS

    def exchange(send, parity):
        return lax.all_to_all(
            send,
            ("dom", "sub"),
            0,
            0,
            axis_index_groups=exchange_groups(sizes, parity),
            tiled=True,
        )

    def assemble(send, later, order, fields):
        shape = one if fields == 1 else two
        recv = exchange(send, order[0])
        send2 = call(
            functools.partial(middle_kernel, sizes, order, fields), shape, recv, later, name="faces"
        )
        return recv, exchange(send2, order[1])

    def shards(geometry, load, cells):
        table = jnp.asarray(apply_table)
        geo, parts, one_hot, send, later = call(
            functools.partial(begin_kernel, sizes, orders[0], square, middle),
            (
                jax.ShapeDtypeStruct(geometry.shape, jnp.bfloat16),
                jax.ShapeDtypeStruct((2, ROWS, LANES), jnp.float32),
                jax.ShapeDtypeStruct((LANES, LANES), jnp.bfloat16),
                two,
                two,
            ),
            *[
                pltpu.with_memory_space_constraint(array, pltpu.HBM)
                for array in (geometry, load, cells, jnp.asarray(diag_table))
            ],
            in_specs=[far] * 4,
            scratch=(
                work,
                pltpu.VMEM(geometry.shape, jnp.bfloat16),
                work,
                pltpu.VMEM(cells.shape, jnp.int32),
                pltpu.VMEM(diag_table.shape, jnp.bfloat16),
                pltpu.SemaphoreType.DMA((4,)),
            ),
            name="begin",
        )
        recv, recv2 = assemble(send, later, orders[0], 2)
        residual, diag, direction, image, send, later = call(
            functools.partial(first_kernel, sizes, orders[0], orders[1], centre),
            (field, field, field, field, one, one),
            parts,
            recv,
            recv2,
            geo,
            table,
            scratch=(work,),
            name="first",
        )
        directions = [direction]
        for step, pair in enumerate(steps[:-1]):
            recv, recv2 = assemble(send, later, orders[step + 1], 1)
            residual, direction, image, send, later = call(
                functools.partial(step_kernel, sizes, orders[step + 1], orders[step + 2], pair),
                (field, field, field, one, one),
                image,
                recv,
                recv2,
                geo,
                table,
                residual,
                diag,
                direction,
                scratch=(work,),
                name="step",
            )
            directions.append(direction)
        recv, recv2 = assemble(send, later, orders[APPLY], 1)
        return call(
            functools.partial(end_kernel, sizes, orders[APPLY], steps[-1]),
            field,
            image,
            recv,
            recv2,
            residual,
            diag,
            *directions,
            one_hot,
            in_specs=[near] * 10,
            out_specs=far,
            scratch=(work, work, pltpu.SemaphoreType.DMA((4,))),
            name="end",
        )

    placed = (P(None, None, ("dom", "sub")), P(None, ("dom", "sub")), P(("dom", "sub"), None))
    return jax.shard_map(
        shards, mesh=mesh, in_specs=placed, out_specs=P(None, ("dom", "sub")), check_vma=False
    )
```

```python
import functools

import jax
import jax.numpy as jnp
import ml_dtypes
import numpy as np
from jax import lax
from jax.experimental import pallas as pl
from jax.experimental.pallas import tpu as pltpu
from jax.sharding import PartitionSpec as P

NP = 8
APPLY = 4
ORDERS = ((0, 1), (1, 0), (0, 1), (1, 0), (0, 1))
LANES = 128
ROWS = NP**3
ROOM = ROWS + 8

cheb_low = 0.4
cheb_high = 4.0


def legendre_values(points, degree):
    before = np.ones(points.shape[0])
    current = points.copy()
    for order in range(2, degree + 1):
        following = ((2 * order - 1) * points * current - (order - 1) * before) / order
        before = current
        current = following
    return (current, before)


def derivative_table(number):
    degree = number - 1
    points = np.cos(np.pi * np.arange(degree + 1) / degree)
    for sweep in range(60):
        current, before = legendre_values(points, degree)
        inner = points[1:-1]
        step_size = (inner * current[1:-1] - before[1:-1]) / ((degree + 1) * current[1:-1])
        points = np.concatenate([points[:1], inner - step_size, points[-1:]])
    points = np.sort(points)
    points = np.concatenate([np.zeros(1) - 1.0, points[1:-1], np.zeros(1) + 1.0])
    values, unused = legendre_values(points, degree)
    matrix = np.zeros((number, number))
    for row_index in range(number):
        for col_index in range(number):
            if row_index != col_index:
                matrix[row_index, col_index] = values[row_index] / (
                    values[col_index] * (points[row_index] - points[col_index])
                )
    matrix[0, 0] = -degree * (degree + 1) / 4.0
    matrix[degree, degree] = degree * (degree + 1) / 4.0
    return matrix


def three_products(matrix):
    matrix = matrix.astype(np.float32)
    high = matrix.astype(ml_dtypes.bfloat16)
    low = (matrix - high.astype(np.float32)).astype(ml_dtypes.bfloat16)
    return np.concatenate([high, high, low], axis=1)


def tables():
    derivative = derivative_table(NP).astype(np.float32).astype(np.float64)
    eye = np.eye(NP)
    inner = three_products(np.kron(eye, derivative))
    inner_t = three_products(np.kron(eye, derivative.T))
    apply_table = np.concatenate([inner, inner_t], axis=0)
    square = derivative * derivative
    diag_table = three_products(np.kron(eye, square.T))
    rows = [[float(v) for v in row] for row in square.T]
    return apply_table, diag_table, rows, [float(v) for v in np.diagonal(derivative)]


def split_rows(values):
    high = values.astype(jnp.bfloat16)
    low = (values - high.astype(jnp.float32)).astype(jnp.bfloat16)
    return jnp.concatenate([high, low, high], axis=0)


def multiply(left, right):
    return jnp.dot(left, right, preferred_element_type=jnp.float32)


def lane_of(rows):
    return lax.broadcasted_iota(jnp.int32, (rows, LANES), 1)


def join_pair(low_face, high_face, lane, unit, number):
    coordinate = (lane // unit) % number
    new_low = low_face + jnp.where(coordinate > 0, pltpu.roll(high_face, unit, 1), 0.0)
    new_high = high_face + jnp.where(
        coordinate < number - 1, pltpu.roll(low_face, LANES - unit, 1), 0.0
    )
    return new_low, new_high


def join_local(ref):
    lane8 = lane_of(8)
    lane64 = lane_of(64)
    for i in range(NP):
        first = slice(i * 64, i * 64 + 8)
        last = slice(i * 64 + 56, i * 64 + 64)
        ref[first, :], ref[last, :] = join_pair(ref[first, :], ref[last, :], lane8, 8, 4)
    ref[0:64, :], ref[448:512, :] = join_pair(ref[0:64, :], ref[448:512, :], lane64, 32, 4)
    first = pl.ds(0, 64, stride=8)
    last = pl.ds(7, 64, stride=8)
    new_first, new_last = join_pair(ref[first, :], ref[last, :], lane64, 1, 8)
    ref[first, :] = new_first
    ref[last, :] = new_last


class Side:
    def __init__(self, sizes, parity):
        a = lax.axis_index("dom")
        b = lax.axis_index("sub")
        last_a = sizes[0] - 1
        last_b = sizes[1] - 1
        self.lr = lax.rem(a + parity, 2)
        self.ls = lax.rem(b + parity, 2)
        self.vr = None
        self.vs = None
        place = 2 * self.lr + self.ls
        dom_step, sub_step = 2, 1
        if parity:
            self.vr = jnp.where(self.lr == 1, a > 0, a < last_a)
            self.vs = jnp.where(self.ls == 1, b > 0, b < last_b)
            row = jnp.logical_or(b == 0, b == last_b)
            column = jnp.logical_or(a == 0, a == last_a)
            rest = jnp.logical_and(a == last_a, b > last_b - 3)
            in_column = ((b + 3) & 3) + jnp.where(rest, 2, 0)
            place = jnp.where(row, (a + 1) & 3, jnp.where(column, in_column, place))
            dom_step = jnp.where(row, 1, 2)
            sub_step = jnp.where(row, 2, 1)
        self.place = place
        self.dom_slot = place ^ dom_step
        self.sub_slot = place ^ sub_step
        self.far_slot = 3 - place
        self.i_row = pl.multiple_of((1 - self.lr) * 448, 64)
        self.j_row = (1 - self.ls) * 56


def keep(mask, *conditions):
    for condition in conditions:
        if condition is not None:
            mask = jnp.logical_and(mask, condition)
    return mask


def pack_faces(ref, side):
    lane = lane_of(16)
    dom_face = jnp.zeros((16, LANES), jnp.float32)
    sub_face = jnp.zeros((16, LANES), jnp.float32)
    for g in range(4):
        block = ref[pl.ds(pl.multiple_of(side.i_row + g * 16, 8), 16), :]
        shift = (g * 32 + 32 * (1 - side.lr)) & 127
        dom_face = jnp.where(lane // 32 == g, pltpu.roll(block, shift, 1), dom_face)
        block = jnp.concatenate(
            [
                ref[pl.ds(pl.multiple_of(i * 64 + side.j_row, 8), 8), :]
                for i in (2 * g, 2 * g + 1)
            ],
            axis=0,
        )
        shift = (g * 8 + 128 - 24 * (1 - side.ls)) & 127
        sub_face = jnp.where((lane // 8) % 4 == g, pltpu.roll(block, shift, 1), sub_face)
    corner = ref[pl.ds(pl.multiple_of(side.i_row + side.j_row, 8), 8), :]
    return dom_face, sub_face, corner


def write_faces(out_ref, field, faces, side):
    dom_face, sub_face, corner = faces
    row = field * 16
    out_ref[side.dom_slot, row : row + 16, :] = dom_face
    out_ref[side.sub_slot, row : row + 16, :] = sub_face
    out_ref[side.far_slot, row : row + 8, :] = corner
    out_ref[side.far_slot, row + 8 : row + 16, :] = jnp.zeros((8, LANES), jnp.float32)
    out_ref[side.place, row : row + 16, :] = jnp.zeros((16, LANES), jnp.float32)


def add_faces(ref, recv_ref, field, side):
    lane = lane_of(16)
    lane8 = lane_of(8)
    row = field * 16
    dom_face = recv_ref[side.dom_slot, row : row + 16, :]
    for g in range(4):
        shift = (96 * (1 - side.lr) + 128 - g * 32) & 127
        mask = keep(lane // 32 == 3 * (1 - side.lr), side.vr)
        at = pl.ds(pl.multiple_of(side.i_row + g * 16, 8), 16)
        ref[at, :] = ref[at, :] + jnp.where(mask, pltpu.roll(dom_face, shift, 1), 0.0)
    sub_mask = keep((lane8 // 8) % 4 == 3 * (1 - side.ls), side.vs)
    sub_face = recv_ref[side.sub_slot, row : row + 16, :]
    for g in range(4):
        shift = (24 * (1 - side.ls) + 128 - g * 8) & 127
        rolled = pltpu.roll(sub_face, shift, 1)
        for part in range(2):
            at = pl.ds(pl.multiple_of((2 * g + part) * 64 + side.j_row, 8), 8)
            piece = rolled[part * 8 : part * 8 + 8, :]
            ref[at, :] = ref[at, :] + jnp.where(sub_mask, piece, 0.0)
    corner = recv_ref[side.far_slot, row : row + 8, :]
    offset = 96 * (1 - side.lr) + 24 * (1 - side.ls)
    shift = (2 * offset + 256 - 120) & 127
    mask = keep(lane8 // 8 == offset // 8, side.vr, side.vs)
    at = pl.ds(pl.multiple_of(side.i_row + side.j_row, 8), 8)
    ref[at, :] = ref[at, :] + jnp.where(mask, pltpu.roll(corner, shift, 1), 0.0)


def halves(matrix):
    flipped = matrix[:, ::-1]
    even = 0.5 * (matrix + flipped)[:4, :4]
    odd = 0.5 * (matrix - flipped)[:4, :4]
    return [[float(v) for v in row] for row in even], [[float(v) for v in row] for row in odd]


def blend(parts, matrix):
    out = []
    for row in matrix:
        total = parts[0] * row[0]
        for a in range(1, NP):
            total = total + parts[a] * row[a]
        out.append(total)
    return out


def derive(parts, pair):
    even, odd = pair
    sums = [parts[a] + parts[7 - a] for a in range(4)]
    gaps = [parts[a] - parts[7 - a] for a in range(4)]
    low = []
    high = []
    for i in range(4):
        first = sums[0] * even[i][0]
        second = gaps[0] * odd[i][0]
        for a in range(1, 4):
            first = first + sums[a] * even[i][a]
            second = second + gaps[a] * odd[i][a]
        low.append(second + first)
        high.append(second - first)
    return low + high[::-1]


def apply_operator(value_ref, geo_ref, table_ref, image_ref, work_ref):
    forward, backward = PAIRS
    inner = table_ref[0:64, :]
    inner_t = table_ref[64:128, :]
    for j in range(NP):
        rows = [slice(i * 64 + j * 8, i * 64 + j * 8 + 8) for i in range(NP)]
        for at, part in zip(rows, derive([value_ref[at, :] for at in rows], forward)):
            work_ref[at, :] = part
    for i in range(NP):
        at = slice(i * 64, i * 64 + 64)
        rows = [slice(i * 64 + j * 8, i * 64 + j * 8 + 8) for j in range(NP)]
        grad_t = multiply(inner, split_rows(value_ref[at, :]))
        grad_r = work_ref[at, :]
        grad_s = jnp.concatenate(derive([value_ref[row, :] for row in rows], forward), axis=0)
        g = [geo_ref[index, at, :].astype(jnp.float32) for index in range(6)]
        work_ref[at, :] = g[0] * grad_r + g[3] * grad_s + g[4] * grad_t
        flux_s = g[3] * grad_r + g[1] * grad_s + g[5] * grad_t
        flux_t = g[4] * grad_r + g[5] * grad_s + g[2] * grad_t
        from_s = derive([flux_s[j * 8 : j * 8 + 8, :] for j in range(NP)], backward)
        image_ref[at, :] = jnp.concatenate(from_s, axis=0) + multiply(
            inner_t, split_rows(flux_t)
        )
    for j in range(NP):
        rows = [slice(i * 64 + j * 8, i * 64 + j * 8 + 8) for i in range(NP)]
        for at, part in zip(rows, derive([work_ref[at, :] for at in rows], backward)):
            image_ref[at, :] = image_ref[at, :] + part


PAIRS = tuple(
    halves(m) for m in (derivative_table(NP).astype(np.float32), derivative_table(NP).T.astype(np.float32))
)


def emit_faces(ref, field, send_ref, later_ref, sides):
    write_faces(send_ref, field, pack_faces(ref, sides[0]), sides[0])
    write_faces(later_ref, field, pack_faces(ref, sides[1]), sides[1])


def permute_exact(values, table):
    total = None
    for part in range(3):
        piece = values.astype(jnp.bfloat16)
        moved = multiply(piece, table)
        values = values - piece.astype(jnp.float32)
        total = moved if total is None else total + moved
    return total


def begin_kernel(sizes, order, square, middle, geo_hbm, load_hbm, cells_hbm, table_hbm, geo_out, parts_ref, one_hot_ref, send_ref, later_ref, work_ref, geo_ref, load_ref, cells_ref, table_ref, sems):
    copies = [
        pltpu.make_async_copy(source, target, sems.at[index])
        for index, (source, target) in enumerate(
            (
                (cells_hbm, cells_ref),
                (geo_hbm, geo_ref),
                (load_hbm, load_ref),
                (table_hbm, table_ref),
            )
        )
    ]
    for copy in copies:
        copy.start()
    copies[0].wait()
    cell = lax.broadcasted_iota(jnp.int32, (LANES, LANES), 0)
    by_cell = jnp.where(cell == jnp.broadcast_to(cells_ref[...], (LANES, LANES)), 1.0, 0.0)
    one_hot_ref[...] = by_cell.astype(jnp.bfloat16)
    table = by_cell.T.astype(jnp.bfloat16)
    load_part = parts_ref.at[0]
    diag_part = parts_ref.at[1]
    for copy in copies[1:]:
        copy.wait()
    for index in range(6):
        moved = multiply(geo_ref[index], table)
        geo_out[index] = moved.astype(jnp.bfloat16)
        if index == 0:
            work_ref[...] = moved
    inner = table_ref[...]
    for j in range(NP):
        rows = [slice(i * 64 + j * 8, i * 64 + j * 8 + 8) for i in range(NP)]
        for at, part in zip(rows, blend([work_ref[at, :] for at in rows], square)):
            diag_part[at, :] = part
    sub_row = lax.broadcasted_iota(jnp.int32, (64, LANES), 0) % 8
    third = jnp.where(sub_row == 0, middle[0], jnp.where(sub_row == 7, middle[7], 0.0))
    for i in range(NP):
        at = slice(i * 64, i * 64 + 64)
        load_part[at, :] = permute_exact(load_ref[at, :], table)
        second = geo_out[1, at, :].astype(jnp.float32)
        fifth = geo_out[5, at, :].astype(jnp.float32)
        pieces = blend([second[j * 8 : j * 8 + 8, :] for j in range(NP)], square)
        for j in (0, 7):
            extra = middle[j] * third[0:8, :] * fifth[j * 8 : j * 8 + 8, :]
            if i in (0, 7):
                cross = geo_out[3, at, :].astype(jnp.float32)[j * 8 : j * 8 + 8, :]
                extra = extra + middle[i] * middle[j] * cross
            pieces[j] = pieces[j] + 2.0 * extra
        total = jnp.concatenate(pieces, axis=0)
        total = total + multiply(inner, split_rows(geo_out[2, at, :].astype(jnp.float32)))
        if i in (0, 7):
            total = total + 2.0 * middle[i] * third * geo_out[4, at, :].astype(jnp.float32)
        diag_part[at, :] = diag_part[at, :] + total
    sides = two_sides(sizes, order)
    for field in range(2):
        join_local(parts_ref.at[field])
        emit_faces(parts_ref.at[field], field, send_ref, later_ref, sides)


def middle_kernel(sizes, order, fields, recv_ref, later_ref, out_ref):
    now, then = two_sides(sizes, order)
    out_ref[...] = later_ref[...]
    lane = lane_of(8)
    for field in range(fields):
        row = field * 16

        def correct(slot_in, low_in, slot_out, low_out, valid):
            piece = recv_ref[slot_in, pl.ds(pl.multiple_of(row + 8 * (1 - low_in), 8), 8), :]
            shift = (8 + 128 - 8 * (1 - low_out) + 8 * (1 - low_in) - 8) & 127
            mask = keep(lane // 8 == 15 * (1 - low_out), valid)
            at = pl.ds(pl.multiple_of(row + 8 * (1 - low_out), 8), 8)
            out_ref[slot_out, at, :] = out_ref[slot_out, at, :] + jnp.where(
                mask, pltpu.roll(piece, shift, 1), 0.0
            )

        correct(now.sub_slot, then.lr, then.dom_slot, now.ls, now.vs)
        correct(now.dom_slot, then.ls, then.sub_slot, now.lr, now.vr)


def two_sides(sizes, order):
    return Side(sizes, order[0]), Side(sizes, order[1])


def coefficients():
    centre = 0.5 * (cheb_high + cheb_low)
    half_width = 0.5 * (cheb_high - cheb_low)
    ratio = centre / half_width
    rho_now = 1.0 / ratio
    steps = []
    for step in range(APPLY):
        rho_new = 1.0 / (2.0 * ratio - rho_now)
        steps.append((rho_new * rho_now, 2.0 * rho_new / half_width))
        rho_now = rho_new
    return centre, steps


def first_kernel(sizes, before, order, centre, parts_ref, recv_ref, recv2_ref, geo_ref, table_ref, residual_ref, diag_ref, direction_ref, image_ref, send_ref, later_ref, work_ref):
    sides = two_sides(sizes, before)
    residual_ref[...] = parts_ref[0, 0:ROWS, :]
    diag_ref[...] = parts_ref[1, 0:ROWS, :]
    for field, ref in ((0, residual_ref), (1, diag_ref)):
        add_faces(ref, recv_ref, field, sides[0])
        add_faces(ref, recv2_ref, field, sides[1])
    direction_ref[...] = residual_ref[...] / diag_ref[...] / centre
    apply_operator(direction_ref, geo_ref, table_ref, image_ref, work_ref)
    join_local(image_ref)
    emit_faces(image_ref, 0, send_ref, later_ref, two_sides(sizes, order))


def step_kernel(sizes, before, order, pair, part_ref, recv_ref, recv2_ref, geo_ref, table_ref, old_residual_ref, diag_ref, old_direction_ref, residual_ref, direction_ref, image_ref, send_ref, later_ref, work_ref):
    sides = two_sides(sizes, before)
    work_ref[...] = part_ref[0:ROWS, :]
    add_faces(work_ref, recv_ref, 0, sides[0])
    add_faces(work_ref, recv2_ref, 0, sides[1])
    residual = old_residual_ref[...] - work_ref[...]
    residual_ref[...] = residual
    direction_ref[...] = pair[0] * old_direction_ref[...] + pair[1] * (residual / diag_ref[...])
    apply_operator(direction_ref, geo_ref, table_ref, image_ref, work_ref)
    join_local(image_ref)
    emit_faces(image_ref, 0, send_ref, later_ref, two_sides(sizes, order))


def end_kernel(sizes, before, pair, part_ref, recv_ref, recv2_ref, residual_ref, diag_ref, d0_ref, d1_ref, d2_ref, d3_ref, one_hot_ref, out_hbm, work_ref, out_ref, sems):
    sides = two_sides(sizes, before)
    work_ref[...] = part_ref[0:ROWS, :]
    add_faces(work_ref, recv_ref, 0, sides[0])
    add_faces(work_ref, recv2_ref, 0, sides[1])
    table = one_hot_ref[...]
    copies = []
    for i in range(NP):
        at = slice(i * 64, i * 64 + 64)
        residual = residual_ref[at, :] - work_ref[at, :]
        last = d3_ref[at, :]
        direction = pair[0] * last + pair[1] * (residual / diag_ref[at, :])
        iterate = d0_ref[at, :] + d1_ref[at, :] + d2_ref[at, :] + last + direction
        out_ref[at, :] = permute_exact(iterate, table)
        if i % 2 == 1:
            here = pl.ds((i - 1) * 64, 128)
            copy = pltpu.make_async_copy(out_ref.at[here], out_hbm.at[here], sems.at[i // 2])
            copy.start()
            copies.append(copy)
    for copy in copies:
        copy.wait()


def call(kernel, outs, *operands, scratch=(), name=None, **specs):
    return pl.pallas_call(
        kernel,
        out_shape=outs,
        scratch_shapes=list(scratch),
        compiler_params=pltpu.CompilerParams(vmem_limit_bytes=32 * 2**20),
        name=name,
        **specs,
    )(*operands)


def exchange_groups(sizes, parity):
    dom, sub = sizes
    whole = []
    if parity:
        for b in (0, sub - 1):
            whole += [[((a + step) % dom, b) for step in range(4)] for a in range(-1, dom - 1, 4)]
        full = 4 * ((sub - 2) // 4)
        for a in (0, dom - 1):
            whole += [[(a, b + step) for step in range(4)] for b in range(1, 1 + full, 4)]
        whole.append([(a, b) for a in (0, dom - 1) for b in (sub - 3, sub - 2)])
    for a in range(parity, dom - 1, 2):
        for b in range(parity, sub - 1, 2):
            whole.append([(a + da, b + db) for da in (0, 1) for db in (0, 1)])
    return [[a * sub + b for a, b in group] for group in whole]


def solution(mesh):
    sizes = (mesh.shape["dom"], mesh.shape["sub"])
    apply_table, diag_table, square, middle = tables()
    centre, steps = coefficients()
    field = jax.ShapeDtypeStruct((ROWS, LANES), jnp.float32)
    sums = jax.ShapeDtypeStruct((ROOM, LANES), jnp.float32)
    one = jax.ShapeDtypeStruct((4, 16, LANES), jnp.float32)
    two = jax.ShapeDtypeStruct((4, 32, LANES), jnp.float32)

    work = pltpu.VMEM((ROWS, LANES), jnp.float32)
    far = pl.BlockSpec(memory_space=pltpu.HBM)
    near = pl.BlockSpec(memory_space=pltpu.VMEM)
    orders = ORDERS

    def exchange(send, parity):
        return lax.all_to_all(
            send,
            ("dom", "sub"),
            0,
            0,
            axis_index_groups=exchange_groups(sizes, parity),
            tiled=True,
        )

    def assemble(send, later, order, fields):
        shape = one if fields == 1 else two
        recv = exchange(send, order[0])
        send2 = call(
            functools.partial(middle_kernel, sizes, order, fields), shape, recv, later, name="faces"
        )
        return recv, exchange(send2, order[1])

    def shards(geometry, load, cells):
        table = jnp.asarray(apply_table)
        geo, parts, one_hot, send, later = call(
            functools.partial(begin_kernel, sizes, orders[0], square, middle),
            (
                jax.ShapeDtypeStruct(geometry.shape, jnp.bfloat16),
                jax.ShapeDtypeStruct((2, ROOM, LANES), jnp.float32),
                jax.ShapeDtypeStruct((LANES, LANES), jnp.bfloat16),
                two,
                two,
            ),
            *[
                pltpu.with_memory_space_constraint(array, pltpu.HBM)
                for array in (geometry, load, cells, jnp.asarray(diag_table))
            ],
            in_specs=[far] * 4,
            scratch=(
                work,
                pltpu.VMEM(geometry.shape, jnp.bfloat16),
                work,
                pltpu.VMEM(cells.shape, jnp.int32),
                pltpu.VMEM(diag_table.shape, jnp.bfloat16),
                pltpu.SemaphoreType.DMA((4,)),
            ),
            name="begin",
        )
        recv, recv2 = assemble(send, later, orders[0], 2)
        residual, diag, direction, image, send, later = call(
            functools.partial(first_kernel, sizes, orders[0], orders[1], centre),
            (field, field, field, sums, one, one),
            parts,
            recv,
            recv2,
            geo,
            table,
            scratch=(work,),
            name="first",
        )
        directions = [direction]
        for step, pair in enumerate(steps[:-1]):
            recv, recv2 = assemble(send, later, orders[step + 1], 1)
            residual, direction, image, send, later = call(
                functools.partial(step_kernel, sizes, orders[step + 1], orders[step + 2], pair),
                (field, field, sums, one, one),
                image,
                recv,
                recv2,
                geo,
                table,
                residual,
                diag,
                direction,
                scratch=(work,),
                name="step",
            )
            directions.append(direction)
        recv, recv2 = assemble(send, later, orders[APPLY], 1)
        return call(
            functools.partial(end_kernel, sizes, orders[APPLY], steps[-1]),
            field,
            image,
            recv,
            recv2,
            residual,
            diag,
            *directions,
            one_hot,
            in_specs=[near] * 10,
            out_specs=far,
            scratch=(work, work, pltpu.SemaphoreType.DMA((4,))),
            name="end",
        )

    placed = (P(None, None, ("dom", "sub")), P(None, ("dom", "sub")), P(("dom", "sub"), None))
    return jax.shard_map(
        shards, mesh=mesh, in_specs=placed, out_specs=P(None, ("dom", "sub")), check_vma=False
    )
```

```python
import functools

import jax
import jax.numpy as jnp
import ml_dtypes
import numpy as np
from jax import lax
from jax.experimental import pallas as pl
from jax.experimental.pallas import tpu as pltpu
from jax.sharding import PartitionSpec as P

NP = 8
APPLY = 4
ORDERS = ((0, 1), (1, 0), (0, 1), (1, 0), (0, 1))
LANES = 128
ROWS = NP**3
ROOM = ROWS + 8

cheb_low = 0.4
cheb_high = 4.0


def legendre_values(points, degree):
    before = np.ones(points.shape[0])
    current = points.copy()
    for order in range(2, degree + 1):
        following = ((2 * order - 1) * points * current - (order - 1) * before) / order
        before = current
        current = following
    return (current, before)


def derivative_table(number):
    degree = number - 1
    points = np.cos(np.pi * np.arange(degree + 1) / degree)
    for sweep in range(60):
        current, before = legendre_values(points, degree)
        inner = points[1:-1]
        step_size = (inner * current[1:-1] - before[1:-1]) / ((degree + 1) * current[1:-1])
        points = np.concatenate([points[:1], inner - step_size, points[-1:]])
    points = np.sort(points)
    points = np.concatenate([np.zeros(1) - 1.0, points[1:-1], np.zeros(1) + 1.0])
    values, unused = legendre_values(points, degree)
    matrix = np.zeros((number, number))
    for row_index in range(number):
        for col_index in range(number):
            if row_index != col_index:
                matrix[row_index, col_index] = values[row_index] / (
                    values[col_index] * (points[row_index] - points[col_index])
                )
    matrix[0, 0] = -degree * (degree + 1) / 4.0
    matrix[degree, degree] = degree * (degree + 1) / 4.0
    return matrix


def three_products(matrix):
    matrix = matrix.astype(np.float32)
    high = matrix.astype(ml_dtypes.bfloat16)
    low = (matrix - high.astype(np.float32)).astype(ml_dtypes.bfloat16)
    return np.concatenate([high, high, low], axis=1)


def tables():
    derivative = derivative_table(NP).astype(np.float32).astype(np.float64)
    eye = np.eye(NP)
    inner = three_products(np.kron(eye, derivative))
    inner_t = three_products(np.kron(eye, derivative.T))
    apply_table = np.concatenate([inner, inner_t], axis=0)
    square = derivative * derivative
    diag_table = three_products(np.kron(eye, square.T))[:, ROWS // 8 :]
    rows = [[float(v) for v in row] for row in square.T]
    return apply_table, diag_table, rows, [float(v) for v in np.diagonal(derivative)]


def split_rows(values):
    high = values.astype(jnp.bfloat16)
    low = (values - high.astype(jnp.float32)).astype(jnp.bfloat16)
    return jnp.concatenate([high, low, high], axis=0)


def multiply(left, right):
    return jnp.dot(left, right, preferred_element_type=jnp.float32)


def lane_of(rows):
    return lax.broadcasted_iota(jnp.int32, (rows, LANES), 1)


def join_pair(low_face, high_face, lane, unit, number):
    coordinate = (lane // unit) % number
    new_low = low_face + jnp.where(coordinate > 0, pltpu.roll(high_face, unit, 1), 0.0)
    new_high = high_face + jnp.where(
        coordinate < number - 1, pltpu.roll(low_face, LANES - unit, 1), 0.0
    )
    return new_low, new_high


def join_local(ref):
    lane8 = lane_of(8)
    lane64 = lane_of(64)
    for i in range(NP):
        first = slice(i * 64, i * 64 + 8)
        last = slice(i * 64 + 56, i * 64 + 64)
        ref[first, :], ref[last, :] = join_pair(ref[first, :], ref[last, :], lane8, 8, 4)
    ref[0:64, :], ref[448:512, :] = join_pair(ref[0:64, :], ref[448:512, :], lane64, 32, 4)
    first = pl.ds(0, 64, stride=8)
    last = pl.ds(7, 64, stride=8)
    new_first, new_last = join_pair(ref[first, :], ref[last, :], lane64, 1, 8)
    ref[first, :] = new_first
    ref[last, :] = new_last


class Side:
    def __init__(self, sizes, parity):
        a = lax.axis_index("dom")
        b = lax.axis_index("sub")
        last_a = sizes[0] - 1
        last_b = sizes[1] - 1
        self.lr = lax.rem(a + parity, 2)
        self.ls = lax.rem(b + parity, 2)
        self.vr = None
        self.vs = None
        place = 2 * self.lr + self.ls
        dom_step, sub_step = 2, 1
        if parity:
            self.vr = jnp.where(self.lr == 1, a > 0, a < last_a)
            self.vs = jnp.where(self.ls == 1, b > 0, b < last_b)
            row = jnp.logical_or(b == 0, b == last_b)
            column = jnp.logical_or(a == 0, a == last_a)
            rest = jnp.logical_and(a == last_a, b > last_b - 3)
            in_column = ((b + 3) & 3) + jnp.where(rest, 2, 0)
            place = jnp.where(row, (a + 1) & 3, jnp.where(column, in_column, place))
            dom_step = jnp.where(row, 1, 2)
            sub_step = jnp.where(row, 2, 1)
        self.place = place
        self.dom_slot = place ^ dom_step
        self.sub_slot = place ^ sub_step
        self.far_slot = 3 - place
        self.i_row = pl.multiple_of((1 - self.lr) * 448, 64)
        self.j_row = (1 - self.ls) * 56


def keep(mask, *conditions):
    for condition in conditions:
        if condition is not None:
            mask = jnp.logical_and(mask, condition)
    return mask


def pack_faces(ref, side):
    lane = lane_of(16)
    dom_face = jnp.zeros((16, LANES), jnp.float32)
    sub_face = jnp.zeros((16, LANES), jnp.float32)
    for g in range(4):
        block = ref[pl.ds(pl.multiple_of(side.i_row + g * 16, 8), 16), :]
        shift = (g * 32 + 32 * (1 - side.lr)) & 127
        dom_face = jnp.where(lane // 32 == g, pltpu.roll(block, shift, 1), dom_face)
        block = jnp.concatenate(
            [
                ref[pl.ds(pl.multiple_of(i * 64 + side.j_row, 8), 8), :]
                for i in (2 * g, 2 * g + 1)
            ],
            axis=0,
        )
        shift = (g * 8 + 128 - 24 * (1 - side.ls)) & 127
        sub_face = jnp.where((lane // 8) % 4 == g, pltpu.roll(block, shift, 1), sub_face)
    corner = ref[pl.ds(pl.multiple_of(side.i_row + side.j_row, 8), 8), :]
    return dom_face, sub_face, corner


def write_faces(out_ref, field, faces, side):
    dom_face, sub_face, corner = faces
    row = field * 16
    out_ref[side.dom_slot, row : row + 16, :] = dom_face
    out_ref[side.sub_slot, row : row + 16, :] = sub_face
    out_ref[side.far_slot, row : row + 8, :] = corner
    out_ref[side.far_slot, row + 8 : row + 16, :] = jnp.zeros((8, LANES), jnp.float32)
    out_ref[side.place, row : row + 16, :] = jnp.zeros((16, LANES), jnp.float32)


def add_faces(ref, recv_ref, field, side):
    lane = lane_of(16)
    lane8 = lane_of(8)
    row = field * 16
    dom_face = recv_ref[side.dom_slot, row : row + 16, :]
    for g in range(4):
        shift = (96 * (1 - side.lr) + 128 - g * 32) & 127
        mask = keep(lane // 32 == 3 * (1 - side.lr), side.vr)
        at = pl.ds(pl.multiple_of(side.i_row + g * 16, 8), 16)
        ref[at, :] = ref[at, :] + jnp.where(mask, pltpu.roll(dom_face, shift, 1), 0.0)
    sub_mask = keep((lane8 // 8) % 4 == 3 * (1 - side.ls), side.vs)
    sub_face = recv_ref[side.sub_slot, row : row + 16, :]
    for g in range(4):
        shift = (24 * (1 - side.ls) + 128 - g * 8) & 127
        rolled = pltpu.roll(sub_face, shift, 1)
        for part in range(2):
            at = pl.ds(pl.multiple_of((2 * g + part) * 64 + side.j_row, 8), 8)
            piece = rolled[part * 8 : part * 8 + 8, :]
            ref[at, :] = ref[at, :] + jnp.where(sub_mask, piece, 0.0)
    corner = recv_ref[side.far_slot, row : row + 8, :]
    offset = 96 * (1 - side.lr) + 24 * (1 - side.ls)
    shift = (2 * offset + 256 - 120) & 127
    mask = keep(lane8 // 8 == offset // 8, side.vr, side.vs)
    at = pl.ds(pl.multiple_of(side.i_row + side.j_row, 8), 8)
    ref[at, :] = ref[at, :] + jnp.where(mask, pltpu.roll(corner, shift, 1), 0.0)


def halves(matrix):
    flipped = matrix[:, ::-1]
    even = 0.5 * (matrix + flipped)[:4, :4]
    odd = 0.5 * (matrix - flipped)[:4, :4]
    return [[float(v) for v in row] for row in even], [[float(v) for v in row] for row in odd]


def blend(parts, matrix):
    out = []
    for row in matrix:
        total = parts[0] * row[0]
        for a in range(1, NP):
            total = total + parts[a] * row[a]
        out.append(total)
    return out


def derive(parts, pair):
    even, odd = pair
    sums = [parts[a] + parts[7 - a] for a in range(4)]
    gaps = [parts[a] - parts[7 - a] for a in range(4)]
    low = []
    high = []
    for i in range(4):
        first = sums[0] * even[i][0]
        second = gaps[0] * odd[i][0]
        for a in range(1, 4):
            first = first + sums[a] * even[i][a]
            second = second + gaps[a] * odd[i][a]
        low.append(second + first)
        high.append(second - first)
    return low + high[::-1]


def apply_operator(value_ref, geo_ref, table_ref, image_ref, work_ref):
    forward, backward = PAIRS
    inner = table_ref[0:64, :]
    inner_t = table_ref[64:128, :]
    for j in range(NP):
        rows = [slice(i * 64 + j * 8, i * 64 + j * 8 + 8) for i in range(NP)]
        for at, part in zip(rows, derive([value_ref[at, :] for at in rows], forward)):
            work_ref[at, :] = part
    for i in range(NP):
        at = slice(i * 64, i * 64 + 64)
        rows = [slice(i * 64 + j * 8, i * 64 + j * 8 + 8) for j in range(NP)]
        grad_t = multiply(inner, split_rows(value_ref[at, :]))
        grad_r = work_ref[at, :]
        grad_s = jnp.concatenate(derive([value_ref[row, :] for row in rows], forward), axis=0)
        g = [geo_ref[index, at, :].astype(jnp.float32) for index in range(6)]
        work_ref[at, :] = g[0] * grad_r + g[3] * grad_s + g[4] * grad_t
        flux_s = g[3] * grad_r + g[1] * grad_s + g[5] * grad_t
        flux_t = g[4] * grad_r + g[5] * grad_s + g[2] * grad_t
        from_s = derive([flux_s[j * 8 : j * 8 + 8, :] for j in range(NP)], backward)
        image_ref[at, :] = jnp.concatenate(from_s, axis=0) + multiply(
            inner_t, split_rows(flux_t)
        )
    for j in range(NP):
        rows = [slice(i * 64 + j * 8, i * 64 + j * 8 + 8) for i in range(NP)]
        for at, part in zip(rows, derive([work_ref[at, :] for at in rows], backward)):
            image_ref[at, :] = image_ref[at, :] + part


PAIRS = tuple(
    halves(m) for m in (derivative_table(NP).astype(np.float32), derivative_table(NP).T.astype(np.float32))
)


def emit_faces(ref, field, send_ref, later_ref, sides):
    write_faces(send_ref, field, pack_faces(ref, sides[0]), sides[0])
    write_faces(later_ref, field, pack_faces(ref, sides[1]), sides[1])


def permute_parts(values, table):
    total = None
    for part in range(2):
        piece = values.astype(jnp.bfloat16)
        moved = multiply(piece, table)
        values = values - piece.astype(jnp.float32)
        total = moved if total is None else total + moved
    return total


def begin_kernel(sizes, order, square, middle, geo_hbm, load_hbm, cells_hbm, table_hbm, geo_out, parts_ref, one_hot_ref, send_ref, later_ref, work_ref, geo_ref, load_ref, cells_ref, table_ref, sems):
    copies = [
        pltpu.make_async_copy(source, target, sems.at[index])
        for index, (source, target) in enumerate(
            (
                (cells_hbm, cells_ref),
                (geo_hbm, geo_ref),
                (load_hbm, load_ref),
                (table_hbm, table_ref),
            )
        )
    ]
    for copy in copies:
        copy.start()
    copies[0].wait()
    cell = lax.broadcasted_iota(jnp.int32, (LANES, LANES), 0)
    by_cell = jnp.where(cell == jnp.broadcast_to(cells_ref[...], (LANES, LANES)), 1.0, 0.0)
    one_hot_ref[...] = by_cell.astype(jnp.bfloat16)
    table = by_cell.T.astype(jnp.bfloat16)
    load_part = parts_ref.at[0]
    diag_part = parts_ref.at[1]
    for copy in copies[1:]:
        copy.wait()
    for index in range(6):
        moved = multiply(geo_ref[index], table)
        geo_out[index] = moved.astype(jnp.bfloat16)
        if index == 0:
            work_ref[...] = moved
    inner = table_ref[...]
    for j in range(NP):
        rows = [slice(i * 64 + j * 8, i * 64 + j * 8 + 8) for i in range(NP)]
        for at, part in zip(rows, blend([work_ref[at, :] for at in rows], square)):
            diag_part[at, :] = part
    sub_row = lax.broadcasted_iota(jnp.int32, (64, LANES), 0) % 8
    third = jnp.where(sub_row == 0, middle[0], jnp.where(sub_row == 7, middle[7], 0.0))
    for i in range(NP):
        at = slice(i * 64, i * 64 + 64)
        load_part[at, :] = permute_parts(load_ref[at, :], table)
        second = geo_out[1, at, :].astype(jnp.float32)
        fifth = geo_out[5, at, :].astype(jnp.float32)
        pieces = blend([second[j * 8 : j * 8 + 8, :] for j in range(NP)], square)
        for j in (0, 7):
            extra = middle[j] * third[0:8, :] * fifth[j * 8 : j * 8 + 8, :]
            if i in (0, 7):
                cross = geo_out[3, at, :].astype(jnp.float32)[j * 8 : j * 8 + 8, :]
                extra = extra + middle[i] * middle[j] * cross
            pieces[j] = pieces[j] + 2.0 * extra
        total = jnp.concatenate(pieces, axis=0)
        along = geo_out[2, at, :]
        total = total + multiply(inner, jnp.concatenate([along, along], axis=0))
        if i in (0, 7):
            total = total + 2.0 * middle[i] * third * geo_out[4, at, :].astype(jnp.float32)
        diag_part[at, :] = diag_part[at, :] + total
    sides = two_sides(sizes, order)
    for field in range(2):
        join_local(parts_ref.at[field])
        emit_faces(parts_ref.at[field], field, send_ref, later_ref, sides)


def middle_kernel(sizes, order, fields, recv_ref, later_ref, out_ref):
    now, then = two_sides(sizes, order)
    out_ref[...] = later_ref[...]
    lane = lane_of(8)
    for field in range(fields):
        row = field * 16

        def correct(slot_in, low_in, slot_out, low_out, valid):
            piece = recv_ref[slot_in, pl.ds(pl.multiple_of(row + 8 * (1 - low_in), 8), 8), :]
            shift = (8 + 128 - 8 * (1 - low_out) + 8 * (1 - low_in) - 8) & 127
            mask = keep(lane // 8 == 15 * (1 - low_out), valid)
            at = pl.ds(pl.multiple_of(row + 8 * (1 - low_out), 8), 8)
            out_ref[slot_out, at, :] = out_ref[slot_out, at, :] + jnp.where(
                mask, pltpu.roll(piece, shift, 1), 0.0
            )

        correct(now.sub_slot, then.lr, then.dom_slot, now.ls, now.vs)
        correct(now.dom_slot, then.ls, then.sub_slot, now.lr, now.vr)


def two_sides(sizes, order):
    return Side(sizes, order[0]), Side(sizes, order[1])


def coefficients():
    centre = 0.5 * (cheb_high + cheb_low)
    half_width = 0.5 * (cheb_high - cheb_low)
    ratio = centre / half_width
    rho_now = 1.0 / ratio
    steps = []
    for step in range(APPLY):
        rho_new = 1.0 / (2.0 * ratio - rho_now)
        steps.append((rho_new * rho_now, 2.0 * rho_new / half_width))
        rho_now = rho_new
    return centre, steps


def first_kernel(sizes, before, order, centre, parts_ref, recv_ref, recv2_ref, geo_ref, table_ref, residual_ref, diag_ref, direction_ref, image_ref, send_ref, later_ref, work_ref):
    sides = two_sides(sizes, before)
    residual_ref[...] = parts_ref[0, 0:ROWS, :]
    diag_ref[...] = parts_ref[1, 0:ROWS, :]
    for field, ref in ((0, residual_ref), (1, diag_ref)):
        add_faces(ref, recv_ref, field, sides[0])
        add_faces(ref, recv2_ref, field, sides[1])
    direction_ref[...] = residual_ref[...] / diag_ref[...] / centre
    apply_operator(direction_ref, geo_ref, table_ref, image_ref, work_ref)
    join_local(image_ref)
    emit_faces(image_ref, 0, send_ref, later_ref, two_sides(sizes, order))


def step_kernel(sizes, before, order, pair, part_ref, recv_ref, recv2_ref, geo_ref, table_ref, old_residual_ref, diag_ref, old_direction_ref, residual_ref, direction_ref, image_ref, send_ref, later_ref, work_ref):
    sides = two_sides(sizes, before)
    work_ref[...] = part_ref[0:ROWS, :]
    add_faces(work_ref, recv_ref, 0, sides[0])
    add_faces(work_ref, recv2_ref, 0, sides[1])
    residual = old_residual_ref[...] - work_ref[...]
    residual_ref[...] = residual
    direction_ref[...] = pair[0] * old_direction_ref[...] + pair[1] * (residual / diag_ref[...])
    apply_operator(direction_ref, geo_ref, table_ref, image_ref, work_ref)
    join_local(image_ref)
    emit_faces(image_ref, 0, send_ref, later_ref, two_sides(sizes, order))


def end_kernel(sizes, before, pair, part_ref, recv_ref, recv2_ref, residual_ref, diag_ref, d0_ref, d1_ref, d2_ref, d3_ref, one_hot_ref, out_hbm, work_ref, out_ref, sems):
    sides = two_sides(sizes, before)
    work_ref[...] = part_ref[0:ROWS, :]
    add_faces(work_ref, recv_ref, 0, sides[0])
    add_faces(work_ref, recv2_ref, 0, sides[1])
    table = one_hot_ref[...]
    copies = []
    for i in range(NP):
        at = slice(i * 64, i * 64 + 64)
        residual = residual_ref[at, :] - work_ref[at, :]
        last = d3_ref[at, :]
        direction = pair[0] * last + pair[1] * (residual / diag_ref[at, :])
        iterate = d0_ref[at, :] + d1_ref[at, :] + d2_ref[at, :] + last + direction
        out_ref[at, :] = permute_parts(iterate, table)
        if i % 2 == 1:
            here = pl.ds((i - 1) * 64, 128)
            copy = pltpu.make_async_copy(out_ref.at[here], out_hbm.at[here], sems.at[i // 2])
            copy.start()
            copies.append(copy)
    for copy in copies:
        copy.wait()


def call(kernel, outs, *operands, scratch=(), name=None, **specs):
    return pl.pallas_call(
        kernel,
        out_shape=outs,
        scratch_shapes=list(scratch),
        compiler_params=pltpu.CompilerParams(vmem_limit_bytes=32 * 2**20),
        name=name,
        **specs,
    )(*operands)


def exchange_groups(sizes, parity):
    dom, sub = sizes
    whole = []
    if parity:
        for b in (0, sub - 1):
            whole += [[((a + step) % dom, b) for step in range(4)] for a in range(-1, dom - 1, 4)]
        full = 4 * ((sub - 2) // 4)
        for a in (0, dom - 1):
            whole += [[(a, b + step) for step in range(4)] for b in range(1, 1 + full, 4)]
        whole.append([(a, b) for a in (0, dom - 1) for b in (sub - 3, sub - 2)])
    for a in range(parity, dom - 1, 2):
        for b in range(parity, sub - 1, 2):
            whole.append([(a + da, b + db) for da in (0, 1) for db in (0, 1)])
    return [[a * sub + b for a, b in group] for group in whole]


def solution(mesh):
    sizes = (mesh.shape["dom"], mesh.shape["sub"])
    apply_table, diag_table, square, middle = tables()
    centre, steps = coefficients()
    field = jax.ShapeDtypeStruct((ROWS, LANES), jnp.float32)
    sums = jax.ShapeDtypeStruct((ROOM, LANES), jnp.float32)
    one = jax.ShapeDtypeStruct((4, 16, LANES), jnp.float32)
    two = jax.ShapeDtypeStruct((4, 32, LANES), jnp.float32)

    work = pltpu.VMEM((ROWS, LANES), jnp.float32)
    far = pl.BlockSpec(memory_space=pltpu.HBM)
    near = pl.BlockSpec(memory_space=pltpu.VMEM)
    orders = ORDERS

    def exchange(send, parity):
        return lax.all_to_all(
            send,
            ("dom", "sub"),
            0,
            0,
            axis_index_groups=exchange_groups(sizes, parity),
            tiled=True,
        )

    def assemble(send, later, order, fields):
        shape = one if fields == 1 else two
        recv = exchange(send, order[0])
        send2 = call(
            functools.partial(middle_kernel, sizes, order, fields), shape, recv, later, name="faces"
        )
        return recv, exchange(send2, order[1])

    def shards(geometry, load, cells):
        table = jnp.asarray(apply_table)
        geo, parts, one_hot, send, later = call(
            functools.partial(begin_kernel, sizes, orders[0], square, middle),
            (
                jax.ShapeDtypeStruct(geometry.shape, jnp.bfloat16),
                jax.ShapeDtypeStruct((2, ROOM, LANES), jnp.float32),
                jax.ShapeDtypeStruct((LANES, LANES), jnp.bfloat16),
                two,
                two,
            ),
            *[
                pltpu.with_memory_space_constraint(array, pltpu.HBM)
                for array in (geometry, load, cells, jnp.asarray(diag_table))
            ],
            in_specs=[far] * 4,
            scratch=(
                work,
                pltpu.VMEM(geometry.shape, jnp.bfloat16),
                work,
                pltpu.VMEM(cells.shape, jnp.int32),
                pltpu.VMEM(diag_table.shape, jnp.bfloat16),
                pltpu.SemaphoreType.DMA((4,)),
            ),
            name="begin",
        )
        recv, recv2 = assemble(send, later, orders[0], 2)
        residual, diag, direction, image, send, later = call(
            functools.partial(first_kernel, sizes, orders[0], orders[1], centre),
            (field, field, field, sums, one, one),
            parts,
            recv,
            recv2,
            geo,
            table,
            scratch=(work,),
            name="first",
        )
        directions = [direction]
        for step, pair in enumerate(steps[:-1]):
            recv, recv2 = assemble(send, later, orders[step + 1], 1)
            residual, direction, image, send, later = call(
                functools.partial(step_kernel, sizes, orders[step + 1], orders[step + 2], pair),
                (field, field, sums, one, one),
                image,
                recv,
                recv2,
                geo,
                table,
                residual,
                diag,
                direction,
                scratch=(work,),
                name="step",
            )
            directions.append(direction)
        recv, recv2 = assemble(send, later, orders[APPLY], 1)
        return call(
            functools.partial(end_kernel, sizes, orders[APPLY], steps[-1]),
            field,
            image,
            recv,
            recv2,
            residual,
            diag,
            *directions,
            one_hot,
            in_specs=[near] * 10,
            out_specs=far,
            scratch=(work, work, pltpu.SemaphoreType.DMA((4,))),
            name="end",
        )

    placed = (P(None, None, ("dom", "sub")), P(None, ("dom", "sub")), P(("dom", "sub"), None))
    return jax.shard_map(
        shards, mesh=mesh, in_specs=placed, out_specs=P(None, ("dom", "sub")), check_vma=False
    )
```
